512 devices in a mesh: shard: 64 (over x, z), tp: 8 (over y, core).
Axes of the slice: x: 4, y: 4, z: 16, core: 2. Of those that a mesh axis runs over, the one named last changes fastest.
Arguments:
- hidden: bfloat16 [32768, 4096], P('shard', 'tp'), may hold values from -48 to 48
- latents: bfloat16 [512, 4096], P(None, 'tp'), may hold values from -4 to 4
- lengths: int32 [64, 4], P('shard'), may hold values from 1 to 256, 512 in all within a row
- probes: int32 [256, 8], P('shard'), may hold values from 0 to 511, as said below
- cluster_slot: int32 [512], replicated, may hold values from 0 to 511, as said below
- slab_sizes: int32 [512], replicated, may hold values from 1 to 128, as said below
- passages: bfloat16 [512, 128, 4096], P('shard', None, 'tp'), may hold values from -6 to 6
Outputs:
- scores: float32 [256, 8, 128], P('shard', None, 'tp')
The draws below stay inside these ranges and needn't reach their ends.
Inputs may be any that keep to these rules, and one draw needn't show every extreme that they name: `slab_sizes`: some cluster holds exactly 128 passages. `cluster_slot`: a permutation of the slots. A query's probes are distinct clusters; of the 32 probes of one pack, at most 4 name clusters whose slots lie on one index of shard (slots i * 8 to (i + 1) * 8 - 1), and exactly 4 do for some index in every pack.
All inputs are finite; a program needn't handle non-finite values.
Results may differ from the reference program's by a relative error of at most 0.009.
Values may be sent and summed in bfloat16 or wider, within the bound.
No kernel may reach another device: no remote copies, remote signals or barrier semaphores. Data moves between devices by JAX's collectives and lax.ppermute only.
A program may use at most 64 MiB of HBM per device.

```python
import math
import jax
import jax.numpy as jnp
import numpy as np
from jax import lax

D = 4096
LAT = 512
HEADS = 8
TOK_DEV = 512
R_DEV = 4
SL_DEV = 8
CAP = 128
NPROBE = 8
HEAD = 512
PACKS = 64
TOKENS = 32768
QUERIES = 256
NCLUS = 512
MOST_LEN = 256


def latent_base(key):
    return jnp.clip(jax.random.normal(jax.random.fold_in(key, 77), (LAT, D), jnp.float32), -4.0, 4.0)


def slot_layout(key):
    return jax.random.permutation(jax.random.fold_in(key, 90), NCLUS).astype(jnp.int32)


def draw_latents(key, part):
    base = latent_base(key)
    return base.astype(jnp.bfloat16)


def draw_hidden(key, part):
    key = jax.random.fold_in(key, 2)
    noise = jnp.clip(jax.random.normal(key, (TOKENS, D), jnp.float32), -4.0, 4.0)
    return noise.astype(jnp.bfloat16)


def draw_cluster_slot(key, part):
    layout = slot_layout(key)
    return layout


def draw_probes(key, part):
    layout = slot_layout(key)
    key = jax.random.fold_in(key, 12)
    inverse = jnp.argsort(layout).astype(jnp.int32)
    most = min(4, SL_DEV)
    least = max(1, most // 2)
    items = R_DEV * NPROBE

    def one_pack(pack):
        pack_key = jax.random.fold_in(key, pack)
        step = jax.random.randint(jax.random.fold_in(pack_key, 1), (), least, most + 1)
        order = jax.random.permutation(jax.random.fold_in(pack_key, 2), items)
        position = jnp.arange(items, dtype=jnp.int32)
        group = jnp.where(position < most, 0, 1 + (position - most) // step)
        rank = jnp.where(position < most, position, (position - most) % step)
        owners = jax.random.permutation(jax.random.fold_in(pack_key, 3), PACKS).astype(jnp.int32)
        owner = jnp.take(owners, group)
        local_table = jax.vmap(lambda g: jax.random.permutation(jax.random.fold_in(pack_key, 100 + g), SL_DEV))(jnp.arange(items))
        local = local_table[group, rank].astype(jnp.int32)
        chosen = jnp.take(inverse, owner * SL_DEV + local)
        placed = jnp.zeros((items,), jnp.int32).at[order].set(chosen)
        return placed.reshape(R_DEV, NPROBE)
    return jax.vmap(one_pack)(jnp.arange(PACKS)).reshape(QUERIES, NPROBE).astype(jnp.int32)


def draw_slab_sizes(key, part):
    key = jax.random.fold_in(key, 3)
    sizes = jax.random.randint(key, (NCLUS,), 1, CAP + 1)
    where_full = jax.random.randint(jax.random.fold_in(key, 4), (), 0, NCLUS)
    return sizes.at[where_full].set(CAP).astype(jnp.int32)


def levels(stream_key, extent, split, smallest, top_value):
    level, own = 1.0, jax.random.fold_in(stream_key, 6)
    for dim, parts in split:
        heights = jnp.exp(jax.random.uniform(jax.random.fold_in(own, dim), (parts,), jnp.float32, smallest / len(split), top_value / len(split)))
        level = level * jnp.repeat(heights, extent[dim] // parts).reshape([-1 if axis == dim else 1 for axis in range(len(extent))])
    return level


def length_profile(amount, total, limit, lean):
    weights = [(1 << 20) // math.isqrt(grade ** lean) + 1 for grade in range(2, amount + 1)]
    rest, counts = total - limit - (amount - 1), [1] * (amount - 1)
    while rest > 0:
        free = [i for i in range(amount - 1) if counts[i] < limit]
        whole, budget = sum([weights[i] for i in free]), rest
        for i in free:
            more = min(limit - counts[i], max(1, budget * weights[i] // whole), rest)
            counts[i] = counts[i] + more
            rest = rest - more
    return np.array([limit] + counts)


def ragged(stream_key, number_of, total, bound, slope):
    if number_of == 2:
        one = jax.random.randint(stream_key, (), max(1, total - bound), min(bound, total - 1) + 1)
        return jnp.stack([one, total - one])
    sizes = jnp.asarray(length_profile(number_of, total, bound, slope), jnp.int32)
    twos = (number_of - 1) // 2
    donor, sink = sizes[1:1 + 2 * twos:2], sizes[2:2 + 2 * twos:2]
    slack = jnp.minimum(donor - 1, bound - sink)
    shifted = jax.random.randint(jax.random.fold_in(stream_key, 1), (twos,), 0, 1 << 20) % (slack + 1)
    sizes = sizes.at[1:1 + 2 * twos:2].set(donor - shifted).at[2:2 + 2 * twos:2].set(sink + shifted)
    return sizes[jax.random.permutation(jax.random.fold_in(stream_key, 2), number_of)]


def gaussian(own_key, extent, spread, bound, shards=(), kind=jnp.bfloat16):
    result = spread * jax.random.normal(own_key, extent, jnp.float32)
    if shards:
        result = result * levels(own_key, extent, shards, -0.22, 0.18)
    return jnp.clip(result, -bound, bound).astype(kind)


def setup_inputs(seed: int = 0) -> dict:
    key_of = jax.random.split(jax.random.key(seed), 8)
    hidden = draw_hidden(jax.random.fold_in(key_of[7], 71), 0)
    latents = draw_latents(jax.random.fold_in(key_of[7], 71), 0)
    lengths = jax.vmap(lambda own: ragged(own, R_DEV, TOK_DEV, MOST_LEN, 2))(jax.random.split(key_of[2], PACKS)).reshape((PACKS, R_DEV)).astype(jnp.int32)
    probes = draw_probes(jax.random.fold_in(key_of[7], 71), 0)
    cluster_slot = draw_cluster_slot(jax.random.fold_in(key_of[7], 71), 0)
    slab_sizes = draw_slab_sizes(jax.random.fold_in(key_of[7], 71), 0)
    passages = gaussian(key_of[6], (NCLUS, CAP, D), 1.0, 6.0, ((0, 64), (2, 8)))
    return dict(hidden=hidden, latents=latents, lengths=lengths, probes=probes, cluster_slot=cluster_slot, slab_sizes=slab_sizes, passages=passages)


def reference(hidden, latents, lengths, probes, cluster_slot, slab_sizes, passages):
    lat = latents.astype(jnp.float32).reshape(LAT, HEADS, HEAD)

    def pool_pack(item):
        hid, lens = item
        x = hid.astype(jnp.float32).reshape(TOK_DEV, HEADS, HEAD)
        logits = jnp.einsum('thd,lhd->htl', x, lat) / math.sqrt(HEAD)
        weights = jax.nn.softmax(logits, axis=-1).astype(jnp.bfloat16)
        attended = jnp.einsum('htl,lhd->thd', weights.astype(jnp.float32), lat)
        attended = attended.reshape(TOK_DEV, D).astype(jnp.bfloat16)
        ends = jnp.cumsum(lens)
        starts = ends - lens
        position = jnp.arange(TOK_DEV, dtype=jnp.int32)
        member = ((position[None, :] >= starts[:, None]) & (position[None, :] < ends[:, None])).astype(jnp.bfloat16)
        summed = jnp.dot(member, attended, preferred_element_type=jnp.float32)
        return summed / lens[:, None].astype(jnp.float32)
    pooled = lax.map(pool_pack, (hidden.reshape(PACKS, TOK_DEV, D), lengths))
    pooled = pooled.reshape(QUERIES, D)
    squares = lax.optimization_barrier(jnp.sum(pooled * pooled, axis=-1, keepdims=True))
    query = (pooled / jnp.sqrt(squares + 1e-06)).astype(jnp.bfloat16)
    slots = jnp.take(cluster_slot, probes)
    sizes = jnp.take(slab_sizes, probes)

    def score_one(item):
        row, slot_row = item
        rows = jnp.take(passages, slot_row, axis=0).astype(jnp.float32)
        return jnp.einsum('d,jcd->jc', row.astype(jnp.float32), rows)
    raw = lax.map(score_one, (query, slots))
    column = jnp.arange(CAP, dtype=jnp.int32)
    valid = column[None, None, :] < sizes[:, :, None]
    return jnp.where(valid, raw, jnp.float32(0.0))
```

```python
import functools
import math

import jax
import jax.numpy as jnp
from jax import lax
from jax.experimental import pallas as pl
from jax.experimental.pallas import tpu as pltpu
from jax.sharding import PartitionSpec as P

MOST = 4
LANES = 128
VMEM = pl.BlockSpec(memory_space=pltpu.VMEM)
SMEM = pl.BlockSpec(memory_space=pltpu.SMEM)
NT = (((1,), (1,)), ((), ()))


def route(probes_ref, slot_ref, count, local_slots, owners):
    for owner in range(owners):
        count[owner] = 0
    found = []
    requests, nprobe = probes_ref.shape
    for query in range(requests):
        for j in range(nprobe):
            cluster = probes_ref[query, j]
            slot = slot_ref[cluster]
            owner = slot // local_slots
            rank = count[owner]
            count[owner] = rank + 1
            row = owner * MOST + jnp.minimum(rank, MOST - 1)
            found.append((query, query * nprobe + j, cluster, row, slot % local_slots))
    return found


def pool_kernel(local_slots, owners, lens_ref, probes_ref, slot_ref, hid_ref, lat_ref, pay_ref, ss_ref, rows, count):
    tokens, width = hid_ref.shape
    requests = probes_ref.shape[0]
    lat = lat_ref[...]
    scale = 1.0 / math.sqrt(width)
    group = 8
    chunk = 256
    row_id = lax.broadcasted_iota(jnp.int32, (group, chunk), 0)
    position = lax.broadcasted_iota(jnp.int32, (group, chunk), 1)
    begin = jnp.zeros((group, chunk), jnp.int32)
    end = jnp.zeros((group, chunk), jnp.int32)
    length_id = lax.broadcasted_iota(jnp.int32, (group, width), 0)
    length = jnp.ones((group, width), jnp.int32)
    start = jnp.int32(0)
    for r in range(requests):
        n = lens_ref[0, r]
        begin = jnp.where(row_id == r, start, begin)
        end = jnp.where(row_id == r, start + n, end)
        length = jnp.where(length_id == r, n, length)
        start = start + n
    total = jnp.zeros((group, lat.shape[0]), jnp.float32)
    for c in range(tokens // chunk):
        hid = hid_ref[c * chunk : (c + 1) * chunk, :]
        logits = lax.dot_general(lat, hid, NT, preferred_element_type=jnp.float32) * scale
        top = jnp.max(logits, axis=0, keepdims=True)
        e = jnp.exp(logits - top)
        w = (e * (1.0 / jnp.sum(e, axis=0, keepdims=True))).astype(jnp.bfloat16)
        here = position + c * chunk
        member = jnp.where((here >= begin) & (here < end), 1.0, 0.0).astype(jnp.bfloat16)
        total = total + lax.dot_general(member, w, NT, preferred_element_type=jnp.float32)
    hi = total.astype(jnp.bfloat16).astype(jnp.float32)
    rest = total - hi
    mid = rest.astype(jnp.bfloat16).astype(jnp.float32)
    parts = jnp.concatenate([hi, mid, rest - mid, jnp.zeros_like(hi)], axis=0).astype(jnp.bfloat16)
    sums = jnp.dot(parts, lat, preferred_element_type=jnp.float32)
    sums = sums[:group] + sums[group : 2 * group] + sums[2 * group : 3 * group]
    pooled = sums / length.astype(jnp.float32)
    ss_ref[...] = jnp.broadcast_to(jnp.sum(pooled * pooled, axis=1, keepdims=True), ss_ref.shape)
    rows[...] = jnp.zeros_like(rows)
    for query, _, _, row, local in route(probes_ref, slot_ref, count, local_slots, owners):
        mark = jnp.full((1, LANES), local.astype(jnp.float32), jnp.float32)
        rows[pl.ds(row, 1), :] = jnp.concatenate([pooled[query : query + 1, :], mark], axis=1)
    pay_ref[...] = rows[...].astype(jnp.bfloat16)


def score_kernel(local_slots, rows_ref, pas_ref, out_ref):
    width = pas_ref.shape[1]
    cap = out_ref.shape[1]
    rows = rows_ref[:, :width]
    mark = rows_ref[:, width:].astype(jnp.float32)
    total = jnp.zeros(out_ref.shape, jnp.float32)
    for s in range(local_slots):
        got = lax.dot_general(rows, pas_ref[s * cap : (s + 1) * cap, :], NT, preferred_element_type=jnp.float32)
        total = total + jnp.where(mark == float(s), got, 0.0)
    out_ref[...] = total


def pick_kernel(local_slots, owners, probes_ref, slot_ref, size_ref, got_ref, ss_ref, out_ref, buf, count):
    requests, nprobe = probes_ref.shape
    items = requests * nprobe
    lane = lax.broadcasted_iota(jnp.int32, (1, LANES), 1)
    buf[...] = jnp.zeros_like(buf)
    for query, item, cluster, row, _ in route(probes_ref, slot_ref, count, local_slots, owners):
        buf[item : item + 1, :] = jnp.where(lane < size_ref[cluster], got_ref[pl.ds(row, 1), :], 0.0)
    for query in range(requests):
        first = items + query * nprobe
        buf[first : first + nprobe, :] = jnp.broadcast_to(ss_ref[query : query + 1, :], (nprobe, LANES))
    out_ref[...] = buf[...].T.reshape(out_ref.shape)


def finish_kernel(items, got_ref, out_ref, buf):
    cap = got_ref.shape[1]
    buf[...] = jnp.zeros_like(buf)
    total = got_ref[0]
    for t in range(1, got_ref.shape[0]):
        total = total + got_ref[t]
    buf[:cap, :] = total
    turned = buf[...].T
    score = turned[:items, :cap] / jnp.sqrt(turned[items : 2 * items, :cap] + 1e-06)
    out_ref[...] = score.reshape(out_ref.shape)


def per_device(shards, tps, hidden, latents, lengths, probes, cluster_slot, slab_sizes, passages):
    width = hidden.shape[1]
    local_slots, cap, _ = passages.shape
    requests, nprobe = probes.shape
    pack_rows = shards * MOST
    f32 = jnp.float32
    payload, squares = pl.pallas_call(
        functools.partial(pool_kernel, local_slots, shards),
        out_shape=(
            jax.ShapeDtypeStruct((pack_rows, width + LANES), jnp.bfloat16),
            jax.ShapeDtypeStruct((8, LANES), f32),
        ),
        in_specs=[SMEM, SMEM, SMEM, VMEM, VMEM],
        out_specs=(VMEM, VMEM),
        scratch_shapes=[pltpu.VMEM((pack_rows, width + LANES), f32), pltpu.SMEM((shards,), jnp.int32)],
        name="pool",
    )(lengths, probes, cluster_slot, hidden, latents)
    rows = lax.all_to_all(payload.reshape(shards, MOST, width + LANES), "shard", 0, 0, tiled=True)
    scores = pl.pallas_call(
        functools.partial(score_kernel, local_slots),
        out_shape=jax.ShapeDtypeStruct((pack_rows, cap), f32),
        in_specs=[VMEM, VMEM],
        out_specs=VMEM,
        name="score",
    )(rows.reshape(pack_rows, width + LANES), passages.reshape(local_slots * cap, width))
    got = lax.all_to_all(scores.reshape(shards, MOST, cap), "shard", 0, 0, tiled=True)
    picked = pl.pallas_call(
        functools.partial(pick_kernel, local_slots, shards),
        out_shape=jax.ShapeDtypeStruct((tps, cap // tps, LANES), f32),
        in_specs=[SMEM, SMEM, SMEM, VMEM, VMEM],
        out_specs=VMEM,
        scratch_shapes=[pltpu.VMEM((LANES, cap), f32), pltpu.SMEM((shards,), jnp.int32)],
        name="pick",
    )(probes, cluster_slot, slab_sizes, got.reshape(pack_rows, cap), squares)
    parts = lax.all_to_all(picked, "tp", 0, 0, tiled=True)
    return pl.pallas_call(
        functools.partial(finish_kernel, requests * nprobe),
        out_shape=jax.ShapeDtypeStruct((requests, nprobe, cap // tps), f32),
        in_specs=[VMEM],
        out_specs=VMEM,
        scratch_shapes=[pltpu.VMEM((LANES, LANES), f32)],
        name="finish",
    )(parts)


def solution(mesh):
    placed = (
        P("shard", "tp"),
        P(None, "tp"),
        P("shard", None),
        P("shard", None),
        P(),
        P(),
        P("shard", None, "tp"),
    )
    return jax.shard_map(
        functools.partial(per_device, mesh.shape["shard"], mesh.shape["tp"]),
        mesh=mesh,
        in_specs=placed,
        out_specs=P("shard", None, "tp"),
        check_vma=False,
    )
```

```python
import functools
import math

import jax
import jax.numpy as jnp
from jax import lax
from jax.experimental import pallas as pl
from jax.experimental.pallas import tpu as pltpu
from jax.sharding import PartitionSpec as P

MOST = 4
LANES = 128
VMEM = pl.BlockSpec(memory_space=pltpu.VMEM)
SMEM = pl.BlockSpec(memory_space=pltpu.SMEM)
NT = (((1,), (1,)), ((), ()))


def pool_kernel(
    local_slots, owners, lens_ref, probes_ref, slot_ref, size_ref, hid_ref, lat_ref,
    pay_ref, ss_ref, route_ref, rows, count,
):
    tokens, width = hid_ref.shape
    requests, nprobe = probes_ref.shape
    pieces = width // LANES
    block = MOST * pieces + MOST // 2
    for owner in range(owners):
        count[owner] = 0
    rows[...] = jnp.zeros_like(rows)
    lane = lax.broadcasted_iota(jnp.int32, (1, LANES), 1)
    places = []
    for query in range(requests):
        for j in range(nprobe):
            cluster = probes_ref[query, j]
            slot = slot_ref[cluster]
            owner = slot // local_slots
            rank = jnp.minimum(count[owner], MOST - 1)
            count[owner] = rank + 1
            route_ref[0, query * nprobe + j] = owner * MOST + rank
            route_ref[1, query * nprobe + j] = size_ref[cluster]
            mark = owner * block + MOST * pieces + rank // 2
            side = (lane // (LANES // 2)) == rank % 2
            local = (slot % local_slots).astype(jnp.float32)
            rows[pl.ds(mark, 1), :] = jnp.where(side, local, rows[pl.ds(mark, 1), :])
            places.append((query, owner * block + rank * pieces))
    lat = lat_ref[...]
    scale = 1.0 / math.sqrt(width)
    group = 8
    chunk = 256
    row_id = lax.broadcasted_iota(jnp.int32, (group, chunk), 0)
    position = lax.broadcasted_iota(jnp.int32, (group, chunk), 1)
    begin = jnp.zeros((group, chunk), jnp.int32)
    end = jnp.zeros((group, chunk), jnp.int32)
    length_id = lax.broadcasted_iota(jnp.int32, (group, width), 0)
    length = jnp.ones((group, width), jnp.int32)
    start = jnp.int32(0)
    for r in range(requests):
        n = lens_ref[0, r]
        begin = jnp.where(row_id == r, start, begin)
        end = jnp.where(row_id == r, start + n, end)
        length = jnp.where(length_id == r, n, length)
        start = start + n
    total = jnp.zeros((group, lat.shape[0]), jnp.float32)
    for c in range(tokens // chunk):
        hid = hid_ref[c * chunk : (c + 1) * chunk, :]
        logits = lax.dot_general(lat, hid, NT, preferred_element_type=jnp.float32) * scale
        top = jnp.max(logits, axis=0, keepdims=True)
        e = jnp.exp(logits - top)
        w = (e * (1.0 / jnp.sum(e, axis=0, keepdims=True))).astype(jnp.bfloat16)
        here = position + c * chunk
        member = jnp.where((here >= begin) & (here < end), 1.0, 0.0).astype(jnp.bfloat16)
        total = total + lax.dot_general(member, w, NT, preferred_element_type=jnp.float32)
    hi = total.astype(jnp.bfloat16).astype(jnp.float32)
    rest = total - hi
    mid = rest.astype(jnp.bfloat16).astype(jnp.float32)
    parts = jnp.concatenate([hi, mid, rest - mid, jnp.zeros_like(hi)], axis=0).astype(jnp.bfloat16)
    sums = jnp.dot(parts, lat, preferred_element_type=jnp.float32)
    sums = sums[:group] + sums[group : 2 * group] + sums[2 * group : 3 * group]
    pooled = sums / length.astype(jnp.float32)
    ss_ref[...] = jnp.broadcast_to(jnp.sum(pooled * pooled, axis=1, keepdims=True), ss_ref.shape)
    for query, place in places:
        for f in range(pieces):
            rows[pl.ds(place + f, 1), :] = pooled[query : query + 1, f * LANES : (f + 1) * LANES]
    pay_ref[...] = rows[...].astype(jnp.bfloat16)


def score_kernel(local_slots, owners, rows_ref, pas_ref, out_ref, rows):
    cap = out_ref.shape[1]
    pieces = pas_ref.shape[1] // LANES
    block = rows_ref.shape[0] // owners
    rows[...] = rows_ref[...].astype(jnp.float32)
    lane = lax.broadcasted_iota(jnp.int32, (owners, LANES), 1)
    query = []
    mark = []
    for k in range(MOST):
        piece = [rows[pl.ds(k * pieces + f, owners, stride=block), :] for f in range(pieces)]
        query.append(jnp.concatenate(piece, axis=1))
        own = rows[pl.ds(MOST * pieces + k // 2, owners, stride=block), :]
        side = (lane // (LANES // 2)) == k % 2
        mark.append(jnp.where(side, own, pltpu.roll(own, LANES // 2, 1)))
    query = jnp.concatenate(query, axis=0).astype(jnp.bfloat16)
    mark = jnp.concatenate(mark, axis=0)
    total = jnp.zeros(out_ref.shape, jnp.float32)
    for s in range(local_slots):
        got = lax.dot_general(query, pas_ref[s * cap : (s + 1) * cap, :], NT, preferred_element_type=jnp.float32)
        total = total + jnp.where(mark == float(s), got, 0.0)
    for k in range(MOST):
        out_ref[pl.ds(k, owners, stride=MOST), :] = total[k * owners : (k + 1) * owners]


def pick_kernel(requests, route_ref, got_ref, ss_ref, out_ref, buf):
    items = route_ref.shape[1]
    nprobe = items // requests
    lane = lax.broadcasted_iota(jnp.int32, (1, LANES), 1)
    buf[2 * items :, :] = jnp.zeros((LANES - 2 * items, buf.shape[1]), jnp.float32)
    for item in range(items):
        buf[item : item + 1, :] = jnp.where(lane < route_ref[1, item], got_ref[pl.ds(route_ref[0, item], 1), :], 0.0)
    for query in range(requests):
        first = items + query * nprobe
        buf[first : first + nprobe, :] = jnp.broadcast_to(ss_ref[query : query + 1, :], (nprobe, LANES))
    out_ref[...] = buf[...].T.reshape(out_ref.shape)


def finish_kernel(items, got_ref, out_ref, buf):
    cap = got_ref.shape[1]
    buf[cap:, :] = jnp.zeros((LANES - cap, LANES), jnp.float32)
    total = got_ref[0]
    for t in range(1, got_ref.shape[0]):
        total = total + got_ref[t]
    buf[:cap, :] = total
    turned = buf[...].T
    score = turned[:items, :cap] / jnp.sqrt(turned[items : 2 * items, :cap] + 1e-06)
    out_ref[...] = score.reshape(out_ref.shape)


def pool(local_slots, owners, lengths, probes, cluster_slot, slab_sizes, hidden, latents):
    width = hidden.shape[1]
    block = MOST * (width // LANES) + MOST // 2
    f32 = jnp.float32
    return pl.pallas_call(
        functools.partial(pool_kernel, local_slots, owners),
        out_shape=(
            jax.ShapeDtypeStruct((owners * block, LANES), jnp.bfloat16),
            jax.ShapeDtypeStruct((8, LANES), f32),
            jax.ShapeDtypeStruct((2, probes.size), jnp.int32),
        ),
        in_specs=[SMEM, SMEM, SMEM, SMEM, VMEM, VMEM],
        out_specs=(VMEM, VMEM, SMEM),
        scratch_shapes=[pltpu.VMEM((owners * block, LANES), f32), pltpu.SMEM((owners,), jnp.int32)],
        name="pool",
    )(lengths, probes, cluster_slot, slab_sizes, hidden, latents)


def score(owners, rows, passages):
    local_slots, cap, width = passages.shape
    return pl.pallas_call(
        functools.partial(score_kernel, local_slots, owners),
        out_shape=jax.ShapeDtypeStruct((owners * MOST, cap), jnp.float32),
        in_specs=[VMEM, VMEM],
        out_specs=VMEM,
        scratch_shapes=[pltpu.VMEM(rows.shape, jnp.float32)],
        name="score",
    )(rows, passages.reshape(local_slots * cap, width))


def pick(tps, requests, route, got, squares):
    cap = got.shape[1]
    return pl.pallas_call(
        functools.partial(pick_kernel, requests),
        out_shape=jax.ShapeDtypeStruct((tps, cap // tps, LANES), jnp.float32),
        in_specs=[SMEM, VMEM, VMEM],
        out_specs=VMEM,
        scratch_shapes=[pltpu.VMEM((LANES, cap), jnp.float32)],
        name="pick",
    )(route, got, squares)


def finish(requests, nprobe, parts):
    return pl.pallas_call(
        functools.partial(finish_kernel, requests * nprobe),
        out_shape=jax.ShapeDtypeStruct((requests, nprobe, parts.shape[1]), jnp.float32),
        in_specs=[VMEM],
        out_specs=VMEM,
        scratch_shapes=[pltpu.VMEM((LANES, LANES), jnp.float32)],
        name="finish",
    )(parts)


def per_device(shards, tps, hidden, latents, lengths, probes, cluster_slot, slab_sizes, passages):
    local_slots, cap, _ = passages.shape
    requests, nprobe = probes.shape
    payload, squares, route = pool(
        local_slots, shards, lengths, probes, cluster_slot, slab_sizes, hidden, latents
    )
    blocks = payload.reshape(shards, -1, 2, LANES)
    rows = lax.all_to_all(blocks, "shard", 0, 0, tiled=True).reshape(payload.shape)
    scores = score(shards, rows, passages)
    got = lax.all_to_all(scores.reshape(shards, 1, MOST * cap), "shard", 0, 0, tiled=True)
    picked = pick(tps, requests, route, got.reshape(scores.shape), squares)
    parts = lax.all_to_all(picked, "tp", 0, 0, tiled=True)
    return finish(requests, nprobe, parts)


def solution(mesh):
    placed = (
        P("shard", "tp"),
        P(None, "tp"),
        P("shard", None),
        P("shard", None),
        P(),
        P(),
        P("shard", None, "tp"),
    )
    return jax.shard_map(
        functools.partial(per_device, mesh.shape["shard"], mesh.shape["tp"]),
        mesh=mesh,
        in_specs=placed,
        out_specs=P("shard", None, "tp"),
        check_vma=False,
    )
```

```python
import functools
import math

import jax
import jax.numpy as jnp
from jax import lax
from jax.experimental import pallas as pl
from jax.experimental.pallas import tpu as pltpu
from jax.sharding import PartitionSpec as P

MOST = 4
LANES = 128
GROUP = 8
VMEM = pl.BlockSpec(memory_space=pltpu.VMEM)
SMEM = pl.BlockSpec(memory_space=pltpu.SMEM)
HBM = pl.BlockSpec(memory_space=pltpu.HBM)
NT = (((1,), (1,)), ((), ()))
PARAMS = pltpu.CompilerParams(vmem_limit_bytes=16 << 20)


def pool_kernel(
    local_slots, owners, lens_hbm, probes_hbm, slot_hbm, size_hbm, hid_hbm, lat_hbm,
    pay_ref, ss_ref, route_ref,
    halves, count, code, lens_ref, probes_ref, slot_ref, size_ref, hid_ref, lat_ref, sems,
):
    tokens, width = hid_ref.shape
    requests, nprobe = probes_ref.shape
    pieces = width // LANES
    pairs = pieces // 2
    bits = local_slots.bit_length() - 1
    copies = [
        pltpu.make_async_copy(source, target, sems.at[i])
        for i, (source, target) in enumerate(
            [
                (probes_hbm, probes_ref),
                (slot_hbm, slot_ref),
                (lens_hbm, lens_ref),
                (size_hbm, size_ref),
                (lat_hbm, lat_ref),
                (hid_hbm, hid_ref),
            ]
        )
    ]
    for copy in copies:
        copy.start()
    for owner in range(owners):
        count[owner] = 0
        code[owner] = 0
    pay_ref[...] = jnp.zeros_like(pay_ref)
    for copy in copies:
        copy.wait()

    places = []
    for query in range(requests):
        for j in range(nprobe):
            item = query * nprobe + j
            cluster = probes_ref[query, j]
            slot = slot_ref[cluster]
            owner = lax.shift_right_logical(slot, bits)
            rank = jnp.minimum(count[owner], MOST - 1)
            count[owner] = rank + 1
            code[owner] = code[owner] | ((slot & (local_slots - 1)) << (bits * rank))
            route_ref[0, item] = owner * MOST + rank
            route_ref[1, item] = size_ref[cluster]
            places.append((query, owner, rank))
    side = lax.broadcasted_iota(jnp.int32, (2, LANES), 0)
    half = bits * MOST // 2
    for _, owner, _ in places:
        both = code[owner]
        mark = jnp.where(side == 0, both & ((1 << half) - 1), lax.shift_right_logical(both, half))
        pay_ref[owner, MOST * pairs] = mark.astype(jnp.float32).astype(jnp.bfloat16)

    row_id = lax.broadcasted_iota(jnp.int32, (GROUP, tokens), 0)
    position = lax.broadcasted_iota(jnp.int32, (GROUP, tokens), 1)
    begin = jnp.zeros((GROUP, tokens), jnp.int32)
    end = jnp.zeros((GROUP, tokens), jnp.int32)
    length_id = lax.broadcasted_iota(jnp.int32, (GROUP, width), 0)
    length = jnp.ones((GROUP, width), jnp.int32)
    start = jnp.int32(0)
    for r in range(requests):
        n = lens_ref[0, r]
        begin = jnp.where(row_id == r, start, begin)
        end = jnp.where(row_id == r, start + n, end)
        length = jnp.where(length_id == r, n, length)
        start = start + n
    member = jnp.where((position >= begin) & (position < end), 1.0, 0.0).astype(jnp.bfloat16)
    lat = lat_ref[...]
    logits = lax.dot_general(hid_ref[...], lat, NT, preferred_element_type=jnp.float32)
    top = jnp.max(logits, axis=1, keepdims=True)
    e = jnp.exp2((logits - top) * (math.log2(math.e) / math.sqrt(width)))
    weights = (e * (1.0 / jnp.sum(e, axis=1, keepdims=True))).astype(jnp.bfloat16)
    total = jnp.dot(member, weights, preferred_element_type=jnp.float32)
    hi = total.astype(jnp.bfloat16).astype(jnp.float32)
    rest = total - hi
    mid = rest.astype(jnp.bfloat16).astype(jnp.float32)
    parts = jnp.concatenate([hi, mid, rest - mid, jnp.zeros_like(hi)], axis=0).astype(jnp.bfloat16)
    sums = jnp.dot(parts, lat, preferred_element_type=jnp.float32)
    sums = sums[:GROUP] + sums[GROUP : 2 * GROUP] + sums[2 * GROUP : 3 * GROUP]
    pooled = sums / length.astype(jnp.float32)
    ss_ref[...] = jnp.broadcast_to(jnp.sum(pooled * pooled, axis=1, keepdims=True), ss_ref.shape)

    for query in range(requests):
        for f in range(pieces):
            halves[query * pairs + f // 2, f % 2 : f % 2 + 1, :] = pooled[
                query : query + 1, f * LANES : (f + 1) * LANES
            ]
    row = [halves[q * pairs : (q + 1) * pairs].astype(jnp.bfloat16) for q in range(requests)]
    for query, owner, rank in places:
        pay_ref[owner, pl.ds(rank * pairs, pairs)] = row[query]


def score_kernel(local_slots, owners, rows_ref, pas_ref, out_ref, rows):
    cap = out_ref.shape[1]
    pieces = pas_ref.shape[1] // LANES
    block = rows_ref.shape[0] // owners
    bits = local_slots.bit_length() - 1
    rows[...] = rows_ref[...].astype(jnp.float32)
    query = []
    local = []
    for k in range(MOST):
        piece = [rows[pl.ds(k * pieces + f, owners, stride=block), :] for f in range(pieces)]
        query.append(jnp.concatenate(piece, axis=1))
        mark = rows[pl.ds(MOST * pieces + k // 2, owners, stride=block), :].astype(jnp.int32)
        local.append(lax.shift_right_logical(mark, bits * (k % 2)) & (local_slots - 1))
    query = jnp.concatenate(query, axis=0).astype(jnp.bfloat16)
    local = jnp.concatenate(local, axis=0)
    total = jnp.zeros(out_ref.shape, jnp.float32)
    for s in range(local_slots):
        got = lax.dot_general(query, pas_ref[s * cap : (s + 1) * cap, :], NT, preferred_element_type=jnp.float32)
        total = total + jnp.where(local == s, got, 0.0)
    for k in range(MOST):
        out_ref[pl.ds(k, owners, stride=MOST), :] = total[k * owners : (k + 1) * owners]


def pick_kernel(requests, route_ref, got_ref, ss_ref, out_ref, buf):
    items = route_ref.shape[1]
    nprobe = items // requests
    lane = lax.broadcasted_iota(jnp.int32, (1, LANES), 1)
    buf[2 * items :, :] = jnp.zeros((LANES - 2 * items, buf.shape[1]), jnp.float32)
    for item in range(items):
        row = got_ref[pl.ds(route_ref[0, item], 1), :]
        buf[item : item + 1, :] = jnp.where(lane < route_ref[1, item], row, 0.0)
    for query in range(requests):
        first = items + query * nprobe
        buf[first : first + nprobe, :] = jnp.broadcast_to(ss_ref[query : query + 1, :], (nprobe, LANES))
    out_ref[...] = buf[...].T.reshape(out_ref.shape)


def finish_kernel(items, got_ref, out_ref, buf):
    cap = got_ref.shape[1]
    buf[cap:, :] = jnp.zeros((LANES - cap, LANES), jnp.float32)
    total = got_ref[0]
    for t in range(1, got_ref.shape[0]):
        total = total + got_ref[t]
    buf[:cap, :] = total
    turned = buf[...].T
    score = turned[:items, :cap] / jnp.sqrt(turned[items : 2 * items, :cap] + 1e-06)
    out_ref[...] = score.reshape(out_ref.shape)


def pool(local_slots, owners, lengths, probes, cluster_slot, slab_sizes, hidden, latents):
    pairs = hidden.shape[1] // LANES // 2
    whole = jnp.int32
    operands = (lengths, probes, cluster_slot, slab_sizes, hidden, latents)
    return pl.pallas_call(
        functools.partial(pool_kernel, local_slots, owners),
        out_shape=(
            jax.ShapeDtypeStruct((owners, MOST * pairs + 1, 2, LANES), jnp.bfloat16),
            jax.ShapeDtypeStruct((GROUP, LANES), jnp.float32),
            jax.ShapeDtypeStruct((2, probes.size), whole),
        ),
        in_specs=[HBM] * len(operands),
        out_specs=(VMEM, VMEM, SMEM),
        scratch_shapes=[
            pltpu.VMEM((probes.shape[0] * pairs, 2, LANES), jnp.float32),
            pltpu.SMEM((owners,), whole),
            pltpu.SMEM((owners,), whole),
            pltpu.SMEM(lengths.shape, whole),
            pltpu.SMEM(probes.shape, whole),
            pltpu.SMEM(cluster_slot.shape, whole),
            pltpu.SMEM(slab_sizes.shape, whole),
            pltpu.VMEM(hidden.shape, hidden.dtype),
            pltpu.VMEM(latents.shape, latents.dtype),
            pltpu.SemaphoreType.DMA((len(operands),)),
        ],
        name="pool",
        compiler_params=PARAMS,
    )(*(pltpu.with_memory_space_constraint(x, pltpu.HBM) for x in operands))


def score(owners, rows, passages):
    local_slots, cap, width = passages.shape
    return pl.pallas_call(
        functools.partial(score_kernel, local_slots, owners),
        out_shape=jax.ShapeDtypeStruct((owners * MOST, cap), jnp.float32),
        in_specs=[VMEM, VMEM],
        out_specs=VMEM,
        scratch_shapes=[pltpu.VMEM(rows.shape, jnp.float32)],
        name="score",
        compiler_params=PARAMS,
    )(rows, passages.reshape(local_slots * cap, width))


def pick(tps, requests, route, got, squares):
    cap = got.shape[1]
    return pl.pallas_call(
        functools.partial(pick_kernel, requests),
        out_shape=jax.ShapeDtypeStruct((tps, cap // tps, LANES), jnp.float32),
        in_specs=[SMEM, VMEM, VMEM],
        out_specs=VMEM,
        scratch_shapes=[pltpu.VMEM((LANES, cap), jnp.float32)],
        name="pick",
        compiler_params=PARAMS,
    )(route, got, squares)


def finish(requests, nprobe, parts):
    return pl.pallas_call(
        functools.partial(finish_kernel, requests * nprobe),
        out_shape=jax.ShapeDtypeStruct((requests, nprobe, parts.shape[1]), jnp.float32),
        in_specs=[VMEM],
        out_specs=VMEM,
        scratch_shapes=[pltpu.VMEM((LANES, LANES), jnp.float32)],
        name="finish",
        compiler_params=PARAMS,
    )(parts)


def per_device(shards, tps, hidden, latents, lengths, probes, cluster_slot, slab_sizes, passages):
    local_slots, cap, _ = passages.shape
    requests, nprobe = probes.shape
    payload, squares, route = pool(
        local_slots, shards, lengths, probes, cluster_slot, slab_sizes, hidden, latents
    )
    rows = lax.all_to_all(payload, "shard", 0, 0, tiled=True)
    scores = score(shards, rows.reshape(-1, LANES), passages)
    got = lax.all_to_all(scores.reshape(shards, 1, MOST * cap), "shard", 0, 0, tiled=True)
    picked = pick(tps, requests, route, got.reshape(scores.shape), squares)
    parts = lax.all_to_all(picked, "tp", 0, 0, tiled=True)
    return finish(requests, nprobe, parts)


def solution(mesh):
    placed = (
        P("shard", "tp"),
        P(None, "tp"),
        P("shard", None),
        P("shard", None),
        P(),
        P(),
        P("shard", None, "tp"),
    )
    return jax.shard_map(
        functools.partial(per_device, mesh.shape["shard"], mesh.shape["tp"]),
        mesh=mesh,
        in_specs=placed,
        out_specs=P("shard", None, "tp"),
        check_vma=False,
    )
```

```python
import functools
import math

import jax
import jax.numpy as jnp
from jax import lax
from jax.experimental import pallas as pl
from jax.experimental.pallas import tpu as pltpu
from jax.sharding import Mesh
from jax.sharding import PartitionSpec as P

MOST = 4
LANES = 128
GROUP = 8
XS = 4
VMEM = pl.BlockSpec(memory_space=pltpu.VMEM)
SMEM = pl.BlockSpec(memory_space=pltpu.SMEM)
HBM = pl.BlockSpec(memory_space=pltpu.HBM)
NT = (((1,), (1,)), ((), ()))
PARAMS = pltpu.CompilerParams(vmem_limit_bytes=16 << 20)


def pool_kernel(
    local_slots, owners, lens_hbm, probes_hbm, slot_hbm, size_hbm, hid_hbm, lat_hbm,
    pay_ref, ss_ref, route_ref,
    halves, count, lens_ref, probes_ref, slot_ref, size_ref, hid_ref, lat_ref, sems,
):
    tokens, width = hid_ref.shape
    requests, nprobe = probes_ref.shape
    pieces = width // LANES
    pairs = pieces // 2
    bits = local_slots.bit_length() - 1
    copies = [
        pltpu.make_async_copy(source, target, sems.at[i])
        for i, (source, target) in enumerate(
            [
                (probes_hbm, probes_ref),
                (slot_hbm, slot_ref),
                (lens_hbm, lens_ref),
                (size_hbm, size_ref),
                (lat_hbm, lat_ref),
                (hid_hbm, hid_ref),
            ]
        )
    ]
    for copy in copies:
        copy.start()
    for owner in range(owners):
        count[owner] = 0
    for copy in copies:
        copy.wait()

    lane = lax.broadcasted_iota(jnp.int32, (2, LANES), 1)
    first = lax.broadcasted_iota(jnp.int32, (2, LANES), 0) == 0
    marks = jnp.full((2, LANES), -1, jnp.int32)
    for query in range(requests):
        for j in range(nprobe):
            item = query * nprobe + j
            cluster = probes_ref[query, j]
            slot = slot_ref[cluster]
            owner = lax.shift_right_logical(slot, bits)
            rank = jnp.minimum(count[owner], MOST - 1)
            count[owner] = rank + 1
            place = owner * MOST + rank
            route_ref[0, item] = place
            route_ref[1, item] = size_ref[cluster]
            code = (query << bits) + (slot & (local_slots - 1))
            marks = jnp.where(lane == item, jnp.where(first, place, code), marks)
    marks = marks.astype(jnp.float32).astype(jnp.bfloat16)

    row_id = lax.broadcasted_iota(jnp.int32, (GROUP, tokens), 0)
    position = lax.broadcasted_iota(jnp.int32, (GROUP, tokens), 1)
    begin = jnp.zeros((GROUP, tokens), jnp.int32)
    end = jnp.zeros((GROUP, tokens), jnp.int32)
    length_id = lax.broadcasted_iota(jnp.int32, (GROUP, width), 0)
    length = jnp.ones((GROUP, width), jnp.int32)
    start = jnp.int32(0)
    for r in range(requests):
        n = lens_ref[0, r]
        begin = jnp.where(row_id == r, start, begin)
        end = jnp.where(row_id == r, start + n, end)
        length = jnp.where(length_id == r, n, length)
        start = start + n
    member = jnp.where((position >= begin) & (position < end), 1.0, 0.0).astype(jnp.bfloat16)
    lat = lat_ref[...]
    logits = lax.dot_general(hid_ref[...], lat, NT, preferred_element_type=jnp.float32)
    top = jnp.max(logits, axis=1, keepdims=True)
    e = jnp.exp2((logits - top) * (math.log2(math.e) / math.sqrt(width)))
    weights = (e * (1.0 / jnp.sum(e, axis=1, keepdims=True))).astype(jnp.bfloat16)
    total = jnp.dot(member, weights, preferred_element_type=jnp.float32)
    hi = total.astype(jnp.bfloat16).astype(jnp.float32)
    rest = total - hi
    mid = rest.astype(jnp.bfloat16).astype(jnp.float32)
    parts = jnp.concatenate([hi, mid, rest - mid, jnp.zeros_like(hi)], axis=0).astype(jnp.bfloat16)
    sums = jnp.dot(parts, lat, preferred_element_type=jnp.float32)
    sums = sums[:GROUP] + sums[GROUP : 2 * GROUP] + sums[2 * GROUP : 3 * GROUP]
    pooled = sums / length.astype(jnp.float32)
    ss_ref[...] = jnp.broadcast_to(jnp.sum(pooled * pooled, axis=1, keepdims=True), ss_ref.shape)

    for query in range(requests):
        for f in range(pieces):
            halves[query * pairs + f // 2, f % 2 : f % 2 + 1, :] = pooled[
                query : query + 1, f * LANES : (f + 1) * LANES
            ]
    rows = halves[...].astype(jnp.bfloat16)
    for place in range(pay_ref.shape[0]):
        pay_ref[place, : requests * pairs] = rows
        pay_ref[place, requests * pairs] = marks


def score_kernel(local_slots, owners, requests, rows_ref, pas_ref, out_ref, rows):
    cap = out_ref.shape[1]
    pieces = pas_ref.shape[1] // LANES
    block = rows_ref.shape[0] // owners
    bits = local_slots.bit_length() - 1
    me = (lax.axis_index(("x", "z")) * MOST).astype(jnp.float32)
    rows[...] = rows_ref[...].astype(jnp.float32)
    place = rows[pl.ds(requests * pieces, owners, stride=block), :]
    code = rows[pl.ds(requests * pieces + 1, owners, stride=block), :]
    mine = jnp.concatenate([jnp.where(place == me + float(k), code, 0.0) for k in range(MOST)], axis=0)
    ones = jnp.ones((LANES, LANES), jnp.bfloat16)
    code = jnp.dot(mine.astype(jnp.bfloat16), ones, preferred_element_type=jnp.float32).astype(jnp.int32)
    pieces_of = [
        [rows[pl.ds(q * pieces + f, owners, stride=block), :] for f in range(pieces)] for q in range(requests)
    ]
    chosen = []
    for k in range(MOST):
        query = lax.shift_right_logical(code[k * owners : (k + 1) * owners], bits)
        piece = []
        for f in range(pieces):
            got = pieces_of[0][f]
            for q in range(1, requests):
                got = jnp.where(query == q, pieces_of[q][f], got)
            piece.append(got)
        chosen.append(jnp.concatenate(piece, axis=1))
    chosen = jnp.concatenate(chosen, axis=0).astype(jnp.bfloat16)
    local = code & (local_slots - 1)
    total = jnp.zeros(out_ref.shape, jnp.float32)
    for s in range(local_slots):
        got = lax.dot_general(chosen, pas_ref[s * cap : (s + 1) * cap, :], NT, preferred_element_type=jnp.float32)
        total = total + jnp.where(local == s, got, 0.0)
    for k in range(MOST):
        out_ref[pl.ds(k, owners, stride=MOST), :] = total[k * owners : (k + 1) * owners]


def pick_kernel(requests, route_ref, got_ref, ss_ref, out_ref, buf):
    items = route_ref.shape[1]
    nprobe = items // requests
    lane = lax.broadcasted_iota(jnp.int32, (1, LANES), 1)
    buf[2 * items :, :] = jnp.zeros((LANES - 2 * items, buf.shape[1]), jnp.float32)
    for item in range(items):
        row = got_ref[pl.ds(route_ref[0, item], 1), :]
        buf[item : item + 1, :] = jnp.where(lane < route_ref[1, item], row, 0.0)
    for query in range(requests):
        first = items + query * nprobe
        buf[first : first + nprobe, :] = jnp.broadcast_to(ss_ref[query : query + 1, :], (nprobe, LANES))
    out_ref[...] = buf[...].T.reshape(out_ref.shape)


def finish_kernel(items, got_ref, out_ref, buf):
    cap = got_ref.shape[1]
    buf[cap:, :] = jnp.zeros((LANES - cap, LANES), jnp.float32)
    total = got_ref[0]
    for t in range(1, got_ref.shape[0]):
        total = total + got_ref[t]
    buf[:cap, :] = total
    turned = buf[...].T
    score = turned[:items, :cap] / jnp.sqrt(turned[items : 2 * items, :cap] + 1e-06)
    out_ref[...] = score.reshape(out_ref.shape)


def pool(local_slots, owners, copies, lengths, probes, cluster_slot, slab_sizes, hidden, latents):
    pairs = hidden.shape[1] // LANES // 2
    whole = jnp.int32
    operands = (lengths, probes, cluster_slot, slab_sizes, hidden, latents)
    return pl.pallas_call(
        functools.partial(pool_kernel, local_slots, owners),
        out_shape=(
            jax.ShapeDtypeStruct((copies, probes.shape[0] * pairs + 1, 2, LANES), jnp.bfloat16),
            jax.ShapeDtypeStruct((GROUP, LANES), jnp.float32),
            jax.ShapeDtypeStruct((2, probes.size), whole),
        ),
        in_specs=[HBM] * len(operands),
        out_specs=(VMEM, VMEM, SMEM),
        scratch_shapes=[
            pltpu.VMEM((probes.shape[0] * pairs, 2, LANES), jnp.float32),
            pltpu.SMEM((owners,), whole),
            pltpu.SMEM(lengths.shape, whole),
            pltpu.SMEM(probes.shape, whole),
            pltpu.SMEM(cluster_slot.shape, whole),
            pltpu.SMEM(slab_sizes.shape, whole),
            pltpu.VMEM(hidden.shape, hidden.dtype),
            pltpu.VMEM(latents.shape, latents.dtype),
            pltpu.SemaphoreType.DMA((len(operands),)),
        ],
        name="pool",
        compiler_params=PARAMS,
    )(*(pltpu.with_memory_space_constraint(x, pltpu.HBM) for x in operands))


def score(owners, requests, rows, passages):
    local_slots, cap, width = passages.shape
    return pl.pallas_call(
        functools.partial(score_kernel, local_slots, owners, requests),
        out_shape=jax.ShapeDtypeStruct((owners * MOST, cap), jnp.float32),
        in_specs=[VMEM, VMEM],
        out_specs=VMEM,
        scratch_shapes=[pltpu.VMEM(rows.shape, jnp.float32)],
        name="score",
        compiler_params=PARAMS,
    )(rows, passages.reshape(local_slots * cap, width))


def pick(tps, requests, route, got, squares):
    cap = got.shape[1]
    return pl.pallas_call(
        functools.partial(pick_kernel, requests),
        out_shape=jax.ShapeDtypeStruct((tps, cap // tps, LANES), jnp.float32),
        in_specs=[SMEM, VMEM, VMEM],
        out_specs=VMEM,
        scratch_shapes=[pltpu.VMEM((LANES, cap), jnp.float32)],
        name="pick",
        compiler_params=PARAMS,
    )(route, got, squares)


def finish(requests, nprobe, parts):
    return pl.pallas_call(
        functools.partial(finish_kernel, requests * nprobe),
        out_shape=jax.ShapeDtypeStruct((requests, nprobe, parts.shape[1]), jnp.float32),
        in_specs=[VMEM],
        out_specs=VMEM,
        scratch_shapes=[pltpu.VMEM((LANES, LANES), jnp.float32)],
        name="finish",
        compiler_params=PARAMS,
    )(parts)


def per_device(xs, zs, tps, hidden, latents, lengths, probes, cluster_slot, slab_sizes, passages):
    shards = xs * zs
    local_slots, cap, _ = passages.shape
    requests, nprobe = probes.shape
    payload, squares, route = pool(
        local_slots, shards, zs, lengths, probes, cluster_slot, slab_sizes, hidden, latents
    )
    blocks = lax.all_to_all(payload, "z", 0, 0, tiled=True)
    blocks = jnp.broadcast_to(blocks[None], (xs, *blocks.shape))
    rows = lax.all_to_all(blocks, "x", 0, 0, tiled=True)
    scores = score(shards, requests, rows.reshape(-1, LANES), passages)
    got = lax.all_to_all(scores.reshape(shards, 1, MOST * cap), ("x", "z"), 0, 0, tiled=True)
    picked = pick(tps, requests, route, got.reshape(scores.shape), squares)
    parts = lax.all_to_all(picked, "tp", 0, 0, tiled=True)
    return finish(requests, nprobe, parts)


def solution(mesh):
    tps = mesh.shape["tp"]
    zs = mesh.shape["shard"] // XS
    fine = Mesh(mesh.devices.reshape(XS, zs, tps), ("x", "z", "tp"))
    shard = ("x", "z")
    placed = (
        P(shard, "tp"),
        P(None, "tp"),
        P(shard, None),
        P(shard, None),
        P(),
        P(),
        P(shard, None, "tp"),
    )
    return jax.shard_map(
        functools.partial(per_device, XS, zs, tps),
        mesh=fine,
        in_specs=placed,
        out_specs=P(shard, None, "tp"),
        check_vma=False,
    )
```

```python
import functools
import math

import jax
import jax.numpy as jnp
from jax import lax
from jax.experimental import pallas as pl
from jax.experimental.pallas import tpu as pltpu
from jax.sharding import Mesh
from jax.sharding import PartitionSpec as P

MOST = 4
LANES = 128
GROUP = 8
XS = 4
VMEM = pl.BlockSpec(memory_space=pltpu.VMEM)
SMEM = pl.BlockSpec(memory_space=pltpu.SMEM)
HBM = pl.BlockSpec(memory_space=pltpu.HBM)
NT = (((1,), (1,)), ((), ()))
PARAMS = pltpu.CompilerParams(vmem_limit_bytes=16 << 20)


def pool_kernel(
    local_slots, xs, zs, lens_hbm, probes_hbm, slot_hbm, size_hbm, hid_hbm, lat_hbm,
    pay_ref, ss_ref, route_ref,
    halves, count, lens_ref, probes_ref, slot_ref, size_ref, hid_ref, lat_ref, sems,
):
    tokens, width = hid_ref.shape
    requests, nprobe = probes_ref.shape
    pieces = width // LANES
    pairs = pieces // 2
    bits = local_slots.bit_length() - 1
    copies = [
        pltpu.make_async_copy(source, target, sems.at[i])
        for i, (source, target) in enumerate(
            [
                (probes_hbm, probes_ref),
                (slot_hbm, slot_ref),
                (lens_hbm, lens_ref),
                (size_hbm, size_ref),
                (lat_hbm, lat_ref),
                (hid_hbm, hid_ref),
            ]
        )
    ]
    for copy in copies:
        copy.start()
    for owner in range(xs * zs):
        count[owner] = 0
    for copy in copies:
        copy.wait()

    lane = lax.broadcasted_iota(jnp.int32, (2, LANES), 1)
    first = lax.broadcasted_iota(jnp.int32, (2, LANES), 0) == 0
    marks = jnp.full((2, LANES), -1, jnp.int32)
    for query in range(requests):
        for j in range(nprobe):
            item = query * nprobe + j
            cluster = probes_ref[query, j]
            slot = slot_ref[cluster]
            owner = lax.shift_right_logical(slot, bits)
            rank = jnp.minimum(count[owner], MOST - 1)
            count[owner] = rank + 1
            place = owner * MOST + rank
            x, z = lax.shift_right_logical(owner, zs.bit_length() - 1), owner & (zs - 1)
            group = (x & 1) * MOST + rank
            route_ref[0, item] = group * (zs * xs // 2) + z * (xs // 2) + lax.shift_right_logical(x, 1)
            route_ref[1, item] = size_ref[cluster]
            code = (query << bits) + (slot & (local_slots - 1))
            marks = jnp.where(lane == item, jnp.where(first, place, code), marks)
    marks = marks.astype(jnp.float32).astype(jnp.bfloat16)

    row_id = lax.broadcasted_iota(jnp.int32, (GROUP, tokens), 0)
    position = lax.broadcasted_iota(jnp.int32, (GROUP, tokens), 1)
    begin = jnp.zeros((GROUP, tokens), jnp.int32)
    end = jnp.zeros((GROUP, tokens), jnp.int32)
    length_id = lax.broadcasted_iota(jnp.int32, (GROUP, width), 0)
    length = jnp.ones((GROUP, width), jnp.int32)
    start = jnp.int32(0)
    for r in range(requests):
        n = lens_ref[0, r]
        begin = jnp.where(row_id == r, start, begin)
        end = jnp.where(row_id == r, start + n, end)
        length = jnp.where(length_id == r, n, length)
        start = start + n
    member = jnp.where((position >= begin) & (position < end), 1.0, 0.0).astype(jnp.bfloat16)
    lat = lat_ref[...]
    logits = lax.dot_general(hid_ref[...], lat, NT, preferred_element_type=jnp.float32)
    top = jnp.max(logits, axis=1, keepdims=True)
    e = jnp.exp2((logits - top) * (math.log2(math.e) / math.sqrt(width)))
    weights = (e * (1.0 / jnp.sum(e, axis=1, keepdims=True))).astype(jnp.bfloat16)
    total = jnp.dot(member, weights, preferred_element_type=jnp.float32)
    hi = total.astype(jnp.bfloat16).astype(jnp.float32)
    rest = total - hi
    mid = rest.astype(jnp.bfloat16).astype(jnp.float32)
    parts = jnp.concatenate([hi, mid, rest - mid, jnp.zeros_like(hi)], axis=0).astype(jnp.bfloat16)
    sums = jnp.dot(parts, lat, preferred_element_type=jnp.float32)
    sums = sums[:GROUP] + sums[GROUP : 2 * GROUP] + sums[2 * GROUP : 3 * GROUP]
    pooled = sums / length.astype(jnp.float32)
    ss_ref[...] = jnp.broadcast_to(jnp.sum(pooled * pooled, axis=1, keepdims=True), ss_ref.shape)

    for query in range(requests):
        for f in range(pieces):
            halves[query * pairs + f // 2, f % 2 : f % 2 + 1, :] = pooled[
                query : query + 1, f * LANES : (f + 1) * LANES
            ]
    rows = halves[...].astype(jnp.bfloat16)
    for place in range(pay_ref.shape[0]):
        pay_ref[place, : requests * pairs] = rows
        pay_ref[place, requests * pairs] = marks


def score_kernel(local_slots, xs, zs, requests, rows_ref, pas_ref, ss_ref, out_ref, rows, blocks):
    owners = xs * zs
    cap = LANES
    pieces = pas_ref.shape[1] // LANES
    block = rows_ref.shape[0] // owners
    bits = local_slots.bit_length() - 1
    me = (lax.axis_index(("x", "z")) * MOST).astype(jnp.float32)
    rows[...] = rows_ref[...].astype(jnp.float32)
    place = rows[pl.ds(requests * pieces, owners, stride=block), :]
    code = rows[pl.ds(requests * pieces + 1, owners, stride=block), :]
    mine = jnp.concatenate([jnp.where(place == me + float(k), code, 0.0) for k in range(MOST)], axis=0)
    ones = jnp.ones((LANES, LANES), jnp.bfloat16)
    code = jnp.dot(mine.astype(jnp.bfloat16), ones, preferred_element_type=jnp.float32).astype(jnp.int32)
    pieces_of = [
        [rows[pl.ds(q * pieces + f, owners, stride=block), :] for f in range(pieces)] for q in range(requests)
    ]
    chosen = []
    for k in range(MOST):
        query = lax.shift_right_logical(code[k * owners : (k + 1) * owners], bits)
        piece = []
        for f in range(pieces):
            got = pieces_of[0][f]
            for q in range(1, requests):
                got = jnp.where(query == q, pieces_of[q][f], got)
            piece.append(got)
        chosen.append(jnp.concatenate(piece, axis=1))
    chosen = jnp.concatenate(chosen, axis=0).astype(jnp.bfloat16)
    local = code & (local_slots - 1)
    total = jnp.zeros((MOST * owners, cap), jnp.float32)
    for s in range(local_slots):
        got = lax.dot_general(chosen, pas_ref[s * cap : (s + 1) * cap, :], NT, preferred_element_type=jnp.float32)
        total = total + jnp.where(local == s, got, 0.0)

    tps = zs // GROUP * MOST
    part = LANES // tps
    height = out_ref.shape[0] // (xs * tps)
    lane = lax.broadcasted_iota(jnp.int32, (GROUP, LANES), 1)
    for x in range(xs):
        first = [k * owners + x * zs + h * GROUP for h in range(zs // GROUP) for k in range(MOST)]
        skew = [total[r : r + GROUP] for r in first]
        skew = [pltpu.roll(v, part * g, 1) if g else v for g, v in enumerate(skew)]
        for t in range(tps):
            mixed = skew[0]
            for g in range(1, tps):
                mixed = jnp.where(lane // part == (t + g) % tps, skew[g], mixed)
            mixed = pltpu.roll(mixed, LANES - part * t, 1) if t else mixed
            row = (x * tps + t) * height
            blocks[row : row + GROUP, :] = mixed
    lane = lax.broadcasted_iota(jnp.int32, (1, LANES), 1)
    squares = ss_ref[0:1, :]
    for q in range(1, requests):
        squares = jnp.where(lane % (LANES // 2) // part == q, ss_ref[q : q + 1, :], squares)
    hi = squares.astype(jnp.bfloat16).astype(jnp.float32)
    mid = (squares - hi).astype(jnp.bfloat16).astype(jnp.float32)
    parts = jnp.concatenate([jnp.where(lane < LANES // 2, hi, mid), squares - hi - mid], axis=0)
    for i in range(xs * tps):
        blocks[i * height + GROUP : (i + 1) * height, :] = parts
    out_ref[...] = blocks[...].astype(jnp.bfloat16)


def merge_kernel(xs, tps, got_ref, out_ref, ss_ref, blocks):
    height = blocks.shape[0] // (xs * tps)
    blocks[...] = got_ref[...].astype(jnp.float32)
    total = []
    for x in range(xs):
        acc = blocks[x * tps * height : x * tps * height + GROUP, :]
        for t in range(1, tps):
            row = (x * tps + t) * height
            acc = acc + blocks[row : row + GROUP, :]
        total.append(acc)
    left = lax.broadcasted_iota(jnp.int32, (GROUP, LANES), 1) < LANES // 2
    halves = xs // 2
    for r in range(halves):
        one, two = total[2 * r], total[2 * r + 1]
        near = jnp.where(left, one, pltpu.roll(two, LANES // 2, 1))
        far = jnp.where(left, pltpu.roll(one, LANES // 2, 1), two)
        out_ref[pl.ds(r, GROUP, stride=halves), :] = near
        out_ref[pl.ds(GROUP * halves + r, GROUP, stride=halves), :] = far
    mine = lax.axis_index("x") * (tps * height) + GROUP
    top = blocks[pl.ds(mine, 1), :]
    low = blocks[pl.ds(mine + 1, 1), :]
    for t in range(1, tps):
        top = top + blocks[pl.ds(mine + t * height, 1), :]
        low = low + blocks[pl.ds(mine + t * height + 1, 1), :]
    ss_ref[...] = jnp.broadcast_to(top + pltpu.roll(top, LANES // 2, 1) + low, ss_ref.shape)


def finish_kernel(route_ref, got_ref, ss_ref, out_ref, turned, buf):
    requests, nprobe, part = out_ref.shape
    height = got_ref.shape[0]
    for g in range(LANES // part):
        turned[g * height : (g + 1) * height, :] = pltpu.roll(got_ref[...], LANES - part * g, 1) if g else got_ref[...]
    column = lax.broadcasted_iota(jnp.int32, (1, LANES), 1) + lax.axis_index("tp") * part
    for item in range(requests * nprobe):
        row = turned[pl.ds(route_ref[0, item], 1), :]
        buf[item : item + 1, :] = jnp.where(column < route_ref[1, item], row, 0.0)
    norm = jnp.sqrt(ss_ref[...] + 1e-06)
    for q in range(requests):
        here = pltpu.roll(norm, LANES - part * q, 1) if q else norm
        out_ref[q] = (buf[q * nprobe : (q + 1) * nprobe, :] / here)[:, :part]


def pool(local_slots, xs, zs, lengths, probes, cluster_slot, slab_sizes, hidden, latents):
    pairs = hidden.shape[1] // LANES // 2
    whole = jnp.int32
    operands = (lengths, probes, cluster_slot, slab_sizes, hidden, latents)
    return pl.pallas_call(
        functools.partial(pool_kernel, local_slots, xs, zs),
        out_shape=(
            jax.ShapeDtypeStruct((zs, probes.shape[0] * pairs + 1, 2, LANES), jnp.bfloat16),
            jax.ShapeDtypeStruct((GROUP, LANES), jnp.float32),
            jax.ShapeDtypeStruct((2, probes.size), whole),
        ),
        in_specs=[HBM] * len(operands),
        out_specs=(VMEM, VMEM, SMEM),
        scratch_shapes=[
            pltpu.VMEM((probes.shape[0] * pairs, 2, LANES), jnp.float32),
            pltpu.SMEM((xs * zs,), whole),
            pltpu.SMEM(lengths.shape, whole),
            pltpu.SMEM(probes.shape, whole),
            pltpu.SMEM(cluster_slot.shape, whole),
            pltpu.SMEM(slab_sizes.shape, whole),
            pltpu.VMEM(hidden.shape, hidden.dtype),
            pltpu.VMEM(latents.shape, latents.dtype),
            pltpu.SemaphoreType.DMA((len(operands),)),
        ],
        name="pool",
        compiler_params=PARAMS,
    )(*(pltpu.with_memory_space_constraint(x, pltpu.HBM) for x in operands))


def score(xs, zs, tps, requests, rows, passages, squares):
    local_slots, cap, width = passages.shape
    blocks = (xs * tps * (GROUP + 2), LANES)
    return pl.pallas_call(
        functools.partial(score_kernel, local_slots, xs, zs, requests),
        out_shape=jax.ShapeDtypeStruct(blocks, jnp.bfloat16),
        in_specs=[VMEM, VMEM, VMEM],
        out_specs=VMEM,
        scratch_shapes=[pltpu.VMEM(rows.shape, jnp.float32), pltpu.VMEM(blocks, jnp.float32)],
        name="score",
        compiler_params=PARAMS,
    )(rows, passages.reshape(local_slots * cap, width), squares)


def merge(xs, zs, tps, got):
    return pl.pallas_call(
        functools.partial(merge_kernel, xs, tps),
        out_shape=(
            jax.ShapeDtypeStruct((zs * xs // 2, LANES), jnp.float32),
            jax.ShapeDtypeStruct((GROUP, LANES), jnp.float32),
        ),
        in_specs=[VMEM],
        out_specs=(VMEM, VMEM),
        scratch_shapes=[pltpu.VMEM(got.shape, jnp.float32)],
        name="merge",
        compiler_params=PARAMS,
    )(got)


def finish(requests, nprobe, part, route, got, squares):
    return pl.pallas_call(
        finish_kernel,
        out_shape=jax.ShapeDtypeStruct((requests, nprobe, part), jnp.float32),
        in_specs=[SMEM, VMEM, VMEM],
        out_specs=VMEM,
        scratch_shapes=[
            pltpu.VMEM((LANES // part * got.shape[0], LANES), jnp.float32),
            pltpu.VMEM((requests * nprobe, LANES), jnp.float32),
        ],
        name="finish",
        compiler_params=PARAMS,
    )(route, got, squares)


def per_device(xs, zs, tps, hidden, latents, lengths, probes, cluster_slot, slab_sizes, passages):
    local_slots, cap, _ = passages.shape
    requests, nprobe = probes.shape
    payload, squares, route = pool(
        local_slots, xs, zs, lengths, probes, cluster_slot, slab_sizes, hidden, latents
    )
    blocks = lax.all_to_all(payload, "z", 0, 0, tiled=True)
    blocks = jnp.broadcast_to(blocks[None], (xs, *blocks.shape))
    rows = lax.all_to_all(blocks, "x", 0, 0, tiled=True).reshape(-1, LANES)
    partial = score(xs, zs, tps, requests, rows, passages, squares)
    blocks = lax.all_to_all(partial.reshape(xs * tps, -1, 2, LANES), ("x", "tp"), 0, 0, tiled=True)
    columns, squares = merge(xs, zs, tps, blocks.reshape(partial.shape))
    got = lax.all_to_all(columns.reshape(zs, 1, -1), "z", 0, 0, tiled=True)
    return finish(requests, nprobe, cap // tps, route, got.reshape(columns.shape), squares)


def solution(mesh):
    tps = mesh.shape["tp"]
    zs = mesh.shape["shard"] // XS
    fine = Mesh(mesh.devices.reshape(XS, zs, tps), ("x", "z", "tp"))
    shard = ("x", "z")
    placed = (
        P(shard, "tp"),
        P(None, "tp"),
        P(shard, None),
        P(shard, None),
        P(),
        P(),
        P(shard, None, "tp"),
    )
    return jax.shard_map(
        functools.partial(per_device, XS, zs, tps),
        mesh=fine,
        in_specs=placed,
        out_specs=P(shard, None, "tp"),
        check_vma=False,
    )
```

```python
import functools
import math

import jax
import jax.numpy as jnp
from jax import lax
from jax.experimental import pallas as pl
from jax.experimental.pallas import tpu as pltpu
from jax.sharding import Mesh
from jax.sharding import PartitionSpec as P

MOST = 4
LANES = 128
GROUP = 8
XS = 4
VMEM = pl.BlockSpec(memory_space=pltpu.VMEM)
HBM = pl.BlockSpec(memory_space=pltpu.HBM)
NT = (((1,), (1,)), ((), ()))
PARAMS = pltpu.CompilerParams(vmem_limit_bytes=16 << 20)


def three_parts(value):
    hi = value.astype(jnp.bfloat16).astype(jnp.float32)
    rest = value - hi
    mid = rest.astype(jnp.bfloat16).astype(jnp.float32)
    return hi, mid, rest - mid


def pool_kernel(
    local_slots, xs, zs, tps, lens_hbm, probes_hbm, slot_hbm, size_hbm, hid_hbm, lat_hbm,
    pay_ref, ss_ref, sel_ref,
    halves, count, lens_ref, probes_ref, slot_ref, size_ref, hid_ref, lat_ref, sems,
):
    tokens, width = hid_ref.shape
    requests, nprobe = probes_ref.shape
    pieces = width // LANES
    pairs = pieces // 2
    bits = local_slots.bit_length() - 1
    copies = [
        pltpu.make_async_copy(source, target, sems.at[i])
        for i, (source, target) in enumerate(
            [
                (probes_hbm, probes_ref),
                (slot_hbm, slot_ref),
                (lens_hbm, lens_ref),
                (size_hbm, size_ref),
                (lat_hbm, lat_ref),
                (hid_hbm, hid_ref),
            ]
        )
    ]
    for copy in copies:
        copy.start()
    for owner in range(xs * zs):
        count[owner] = 0
    for copy in copies[:4]:
        copy.wait()

    spot = lax.broadcasted_iota(jnp.int32, (1, LANES), 1)
    part = LANES // tps
    column = (spot & (part - 1)) + lax.axis_index("tp") * part
    group_of = lax.shift_right_logical(spot, part.bit_length() - 1)
    lane = lax.broadcasted_iota(jnp.int32, (2, LANES), 1)
    first = lax.broadcasted_iota(jnp.int32, (2, LANES), 0) == 0
    marks = jnp.full((2, LANES), -1, jnp.int32)
    for query in range(requests):
        for j in range(nprobe):
            item = query * nprobe + j
            cluster = probes_ref[query, j]
            slot = slot_ref[cluster]
            owner = lax.shift_right_logical(slot, bits)
            rank = jnp.minimum(count[owner], MOST - 1)
            count[owner] = rank + 1
            place = owner * MOST + rank
            x, z = lax.shift_right_logical(owner, zs.bit_length() - 1), owner & (zs - 1)
            row = z * (xs // 2) + lax.shift_right_logical(x, 1)
            here = (group_of == (x & 1) * MOST + rank) & (column < size_ref[cluster])
            sel_ref[item : item + 1, :LANES] = jnp.where(spot == row, 1.0, 0.0)
            sel_ref[item : item + 1, LANES:] = jnp.where(here, 1.0, 0.0)
            code = (query << bits) + (slot & (local_slots - 1))
            marks = jnp.where(lane == item, jnp.where(first, place, code), marks)
    marks = marks.astype(jnp.float32).astype(jnp.bfloat16)
    for copy in copies[4:]:
        copy.wait()

    row_id = lax.broadcasted_iota(jnp.int32, (GROUP, tokens), 0)
    position = lax.broadcasted_iota(jnp.int32, (GROUP, tokens), 1)
    begin = jnp.zeros((GROUP, tokens), jnp.int32)
    end = jnp.zeros((GROUP, tokens), jnp.int32)
    length_id = lax.broadcasted_iota(jnp.int32, (GROUP, width), 0)
    length = jnp.ones((GROUP, width), jnp.int32)
    start = jnp.int32(0)
    for r in range(requests):
        n = lens_ref[0, r]
        begin = jnp.where(row_id == r, start, begin)
        end = jnp.where(row_id == r, start + n, end)
        length = jnp.where(length_id == r, n, length)
        start = start + n
    member = jnp.where((position >= begin) & (position < end), 1.0, 0.0).astype(jnp.bfloat16)
    lat = lat_ref[...]
    logits = lax.dot_general(hid_ref[...], lat, NT, preferred_element_type=jnp.float32)
    top = jnp.max(logits, axis=1, keepdims=True)
    e = jnp.exp2((logits - top) * (math.log2(math.e) / math.sqrt(width)))
    weights = (e * (1.0 / jnp.sum(e, axis=1, keepdims=True))).astype(jnp.bfloat16)
    total = jnp.dot(member, weights, preferred_element_type=jnp.float32)
    parts = jnp.concatenate([*three_parts(total), jnp.zeros_like(total)], axis=0).astype(jnp.bfloat16)
    sums = jnp.dot(parts, lat, preferred_element_type=jnp.float32)
    sums = sums[:GROUP] + sums[GROUP : 2 * GROUP] + sums[2 * GROUP : 3 * GROUP]
    pooled = sums / length.astype(jnp.float32)
    ss_ref[...] = jnp.broadcast_to(jnp.sum(pooled * pooled, axis=1, keepdims=True), ss_ref.shape)

    for query in range(requests):
        for f in range(pieces):
            halves[query * pairs + f // 2, f % 2 : f % 2 + 1, :] = pooled[
                query : query + 1, f * LANES : (f + 1) * LANES
            ]
    rows = halves[...].astype(jnp.bfloat16)
    for place in range(pay_ref.shape[0]):
        pay_ref[place, : requests * pairs] = rows
        pay_ref[place, requests * pairs] = marks


def score_kernel(local_slots, xs, zs, requests, rows_ref, pas_ref, ss_ref, out_ref, rows, blocks):
    owners = xs * zs
    cap = LANES
    pieces = pas_ref.shape[1] // LANES
    block = rows_ref.shape[0] // owners
    bits = local_slots.bit_length() - 1
    me = (lax.axis_index(("x", "z")) * MOST).astype(jnp.float32)
    rows[...] = rows_ref[...].astype(jnp.float32)
    place = rows[pl.ds(requests * pieces, owners, stride=block), :]
    code = rows[pl.ds(requests * pieces + 1, owners, stride=block), :]
    mine = jnp.concatenate([jnp.where(place == me + float(k), code, 0.0) for k in range(MOST)], axis=0)
    ones = jnp.ones((LANES, LANES), jnp.bfloat16)
    code = jnp.dot(mine.astype(jnp.bfloat16), ones, preferred_element_type=jnp.float32).astype(jnp.int32)
    pieces_of = [
        [rows[pl.ds(q * pieces + f, owners, stride=block), :] for f in range(pieces)] for q in range(requests)
    ]
    chosen = []
    for k in range(MOST):
        query = lax.shift_right_logical(code[k * owners : (k + 1) * owners], bits)
        piece = []
        for f in range(pieces):
            got = pieces_of[0][f]
            for q in range(1, requests):
                got = jnp.where(query == q, pieces_of[q][f], got)
            piece.append(got)
        chosen.append(jnp.concatenate(piece, axis=1))
    chosen = jnp.concatenate(chosen, axis=0).astype(jnp.bfloat16)
    local = code & (local_slots - 1)
    total = jnp.zeros((MOST * owners, cap), jnp.float32)
    for s in range(local_slots):
        got = lax.dot_general(chosen, pas_ref[s * cap : (s + 1) * cap, :], NT, preferred_element_type=jnp.float32)
        total = total + jnp.where(local == s, got, 0.0)

    tps = zs // GROUP * MOST
    part = LANES // tps
    height = out_ref.shape[0] // (xs * tps)
    lane = lax.broadcasted_iota(jnp.int32, (GROUP, LANES), 1)
    for x in range(xs):
        first = [k * owners + x * zs + h * GROUP for h in range(zs // GROUP) for k in range(MOST)]
        skew = [total[r : r + GROUP] for r in first]
        skew = [pltpu.roll(v, part * g, 1) if g else v for g, v in enumerate(skew)]
        for t in range(tps):
            mixed = skew[0]
            for g in range(1, tps):
                mixed = jnp.where(lane // part == (t + g) % tps, skew[g], mixed)
            mixed = pltpu.roll(mixed, LANES - part * t, 1) if t else mixed
            row = (x * tps + t) * height
            blocks[row : row + GROUP, :] = mixed
    lane = lax.broadcasted_iota(jnp.int32, (1, LANES), 1)
    squares = ss_ref[0:1, :]
    for q in range(1, requests):
        squares = jnp.where(lane % (LANES // 2) // part == q, ss_ref[q : q + 1, :], squares)
    hi, mid, low = three_parts(squares)
    parts = jnp.concatenate([jnp.where(lane < LANES // 2, hi, mid), low], axis=0)
    for i in range(xs * tps):
        blocks[i * height + GROUP : (i + 1) * height, :] = parts
    out_ref[...] = blocks[...].astype(jnp.bfloat16)


def merge_kernel(xs, tps, got_ref, out_ref, ss_ref, blocks):
    height = blocks.shape[0] // (xs * tps)
    blocks[...] = got_ref[...].astype(jnp.float32)
    total = []
    for x in range(xs):
        acc = blocks[x * tps * height : x * tps * height + GROUP, :]
        for t in range(1, tps):
            row = (x * tps + t) * height
            acc = acc + blocks[row : row + GROUP, :]
        total.append(acc)
    left = lax.broadcasted_iota(jnp.int32, (GROUP, LANES), 1) < LANES // 2
    halves = xs // 2
    for r in range(halves):
        one, two = total[2 * r], total[2 * r + 1]
        near = jnp.where(left, one, pltpu.roll(two, LANES // 2, 1))
        far = jnp.where(left, pltpu.roll(one, LANES // 2, 1), two)
        out_ref[pl.ds(r, GROUP, stride=halves), :] = near
        out_ref[pl.ds(GROUP * halves + r, GROUP, stride=halves), :] = far
    mine = lax.axis_index("x") * (tps * height) + GROUP
    top = blocks[pl.ds(mine, 1), :]
    low = blocks[pl.ds(mine + 1, 1), :]
    for t in range(1, tps):
        top = top + blocks[pl.ds(mine + t * height, 1), :]
        low = low + blocks[pl.ds(mine + t * height + 1, 1), :]
    ss_ref[...] = jnp.broadcast_to(top + pltpu.roll(top, LANES // 2, 1) + low, ss_ref.shape)


def finish_kernel(sel_ref, got_ref, ss_ref, out_ref):
    requests, nprobe, part = out_ref.shape
    height = got_ref.shape[0]
    one_hot = sel_ref[:, :height].astype(jnp.bfloat16)
    parts = jnp.concatenate(three_parts(got_ref[...]), axis=1).astype(jnp.bfloat16)
    rows = jnp.dot(one_hot, parts, preferred_element_type=jnp.float32)
    rows = rows[:, :LANES] + rows[:, LANES : 2 * LANES] + rows[:, 2 * LANES :]
    rows = jnp.where(sel_ref[:, LANES:] > 0.0, rows, 0.0)
    step = LANES // 2
    while step >= part:
        rows = rows + pltpu.roll(rows, step, 1)
        step //= 2
    norm = jnp.sqrt(ss_ref[...] + 1e-06)
    for q in range(requests):
        here = pltpu.roll(norm, LANES - part * q, 1) if q else norm
        out_ref[q] = (rows[q * nprobe : (q + 1) * nprobe, :] / here)[:, :part]


def pool(local_slots, xs, zs, tps, lengths, probes, cluster_slot, slab_sizes, hidden, latents):
    pairs = hidden.shape[1] // LANES // 2
    whole = jnp.int32
    operands = (lengths, probes, cluster_slot, slab_sizes, hidden, latents)
    return pl.pallas_call(
        functools.partial(pool_kernel, local_slots, xs, zs, tps),
        out_shape=(
            jax.ShapeDtypeStruct((zs, probes.shape[0] * pairs + 1, 2, LANES), jnp.bfloat16),
            jax.ShapeDtypeStruct((GROUP, LANES), jnp.float32),
            jax.ShapeDtypeStruct((probes.size, 2 * LANES), jnp.float32),
        ),
        in_specs=[HBM] * len(operands),
        out_specs=(VMEM, VMEM, VMEM),
        scratch_shapes=[
            pltpu.VMEM((probes.shape[0] * pairs, 2, LANES), jnp.float32),
            pltpu.SMEM((xs * zs,), whole),
            pltpu.SMEM(lengths.shape, whole),
            pltpu.SMEM(probes.shape, whole),
            pltpu.SMEM(cluster_slot.shape, whole),
            pltpu.SMEM(slab_sizes.shape, whole),
            pltpu.VMEM(hidden.shape, hidden.dtype),
            pltpu.VMEM(latents.shape, latents.dtype),
            pltpu.SemaphoreType.DMA((len(operands),)),
        ],
        name="pool",
        compiler_params=PARAMS,
    )(*(pltpu.with_memory_space_constraint(x, pltpu.HBM) for x in operands))


def score(xs, zs, tps, requests, rows, passages, squares):
    local_slots, cap, width = passages.shape
    blocks = (xs * tps * (GROUP + 2), LANES)
    return pl.pallas_call(
        functools.partial(score_kernel, local_slots, xs, zs, requests),
        out_shape=jax.ShapeDtypeStruct(blocks, jnp.bfloat16),
        in_specs=[VMEM, VMEM, VMEM],
        out_specs=VMEM,
        scratch_shapes=[pltpu.VMEM(rows.shape, jnp.float32), pltpu.VMEM(blocks, jnp.float32)],
        name="score",
        compiler_params=PARAMS,
    )(rows, passages.reshape(local_slots * cap, width), squares)


def merge(xs, zs, tps, got):
    return pl.pallas_call(
        functools.partial(merge_kernel, xs, tps),
        out_shape=(
            jax.ShapeDtypeStruct((zs * xs // 2, LANES), jnp.float32),
            jax.ShapeDtypeStruct((GROUP, LANES), jnp.float32),
        ),
        in_specs=[VMEM],
        out_specs=(VMEM, VMEM),
        scratch_shapes=[pltpu.VMEM(got.shape, jnp.float32)],
        name="merge",
        compiler_params=PARAMS,
    )(got)


def finish(requests, nprobe, part, select, got, squares):
    return pl.pallas_call(
        finish_kernel,
        out_shape=jax.ShapeDtypeStruct((requests, nprobe, part), jnp.float32),
        in_specs=[VMEM, VMEM, VMEM],
        out_specs=VMEM,
        name="finish",
        compiler_params=PARAMS,
    )(select, got, squares)


def per_device(xs, zs, tps, hidden, latents, lengths, probes, cluster_slot, slab_sizes, passages):
    local_slots, cap, _ = passages.shape
    requests, nprobe = probes.shape
    payload, squares, select = pool(
        local_slots, xs, zs, tps, lengths, probes, cluster_slot, slab_sizes, hidden, latents
    )
    blocks = lax.all_to_all(payload, "z", 0, 0, tiled=True)
    blocks = jnp.broadcast_to(blocks[None], (xs, *blocks.shape))
    rows = lax.all_to_all(blocks, "x", 0, 0, tiled=True).reshape(-1, LANES)
    partial = score(xs, zs, tps, requests, rows, passages, squares)
    blocks = lax.all_to_all(partial.reshape(xs * tps, -1, 2, LANES), ("x", "tp"), 0, 0, tiled=True)
    columns, squares = merge(xs, zs, tps, blocks.reshape(partial.shape))
    got = lax.all_to_all(columns.reshape(zs, 1, -1), "z", 0, 0, tiled=True)
    return finish(requests, nprobe, cap // tps, select, got.reshape(columns.shape), squares)


def solution(mesh):
    tps = mesh.shape["tp"]
    zs = mesh.shape["shard"] // XS
    fine = Mesh(mesh.devices.reshape(XS, zs, tps), ("x", "z", "tp"))
    shard = ("x", "z")
    placed = (
        P(shard, "tp"),
        P(None, "tp"),
        P(shard, None),
        P(shard, None),
        P(),
        P(),
        P(shard, None, "tp"),
    )
    return jax.shard_map(
        functools.partial(per_device, XS, zs, tps),
        mesh=fine,
        in_specs=placed,
        out_specs=P(shard, None, "tp"),
        check_vma=False,
    )
```

```python
import functools
import math

import jax
import jax.numpy as jnp
from jax import lax
from jax.experimental import pallas as pl
from jax.experimental.pallas import tpu as pltpu
from jax.sharding import Mesh
from jax.sharding import PartitionSpec as P

MOST = 4
LANES = 128
GROUP = 8
XS = 4
VMEM = pl.BlockSpec(memory_space=pltpu.VMEM)
HBM = pl.BlockSpec(memory_space=pltpu.HBM)
NT = (((1,), (1,)), ((), ()))
PARAMS = pltpu.CompilerParams(vmem_limit_bytes=16 << 20)


def three_parts(value):
    hi = value.astype(jnp.bfloat16).astype(jnp.float32)
    rest = value - hi
    mid = rest.astype(jnp.bfloat16).astype(jnp.float32)
    return hi, mid, rest - mid


def pool_kernel(
    local_slots, xs, zs, tps, lens_hbm, probes_hbm, slot_hbm, size_hbm, hid_hbm, lat_hbm,
    pay_ref, ss_ref, sel_ref,
    halves, count, lens_ref, probes_ref, slot_ref, size_ref, hid_ref, lat_ref, sems,
):
    tokens, width = hid_ref.shape
    requests, nprobe = probes_ref.shape
    pieces = width // LANES
    pairs = pieces // 2
    bits = local_slots.bit_length() - 1
    copies = [
        pltpu.make_async_copy(source, target, sems.at[i])
        for i, (source, target) in enumerate(
            [
                (probes_hbm, probes_ref),
                (slot_hbm, slot_ref),
                (lens_hbm, lens_ref),
                (size_hbm, size_ref),
                (lat_hbm, lat_ref),
                (hid_hbm, hid_ref),
            ]
        )
    ]
    for copy in copies:
        copy.start()
    for owner in range(xs * zs):
        count[owner] = 0
    for copy in copies[:4]:
        copy.wait()

    spot = lax.broadcasted_iota(jnp.int32, (1, LANES), 1)
    part = LANES // tps
    column = (spot & (part - 1)) + lax.axis_index("tp") * part
    group_of = lax.shift_right_logical(spot, part.bit_length() - 1)
    lane = lax.broadcasted_iota(jnp.int32, (2, LANES), 1)
    first = lax.broadcasted_iota(jnp.int32, (2, LANES), 0) == 0
    marks = jnp.full((2, LANES), -1, jnp.int32)
    for query in range(requests):
        for j in range(nprobe):
            item = query * nprobe + j
            cluster = probes_ref[query, j]
            slot = slot_ref[cluster]
            owner = lax.shift_right_logical(slot, bits)
            rank = jnp.minimum(count[owner], MOST - 1)
            count[owner] = rank + 1
            place = owner * MOST + rank
            x, z = lax.shift_right_logical(owner, zs.bit_length() - 1), owner & (zs - 1)
            row = z * (xs // 2) + lax.shift_right_logical(x, 1)
            here = (group_of == (x & 1) * MOST + rank) & (column < size_ref[cluster])
            sel_ref[item : item + 1, :LANES] = jnp.where(spot == row, 1.0, 0.0)
            sel_ref[item : item + 1, LANES:] = jnp.where(here, 1.0, 0.0)
            code = (query << bits) + (slot & (local_slots - 1))
            marks = jnp.where(lane == item, jnp.where(first, place, code), marks)
    marks = marks.astype(jnp.float32).astype(jnp.bfloat16)
    for copy in copies[4:]:
        copy.wait()

    row_id = lax.broadcasted_iota(jnp.int32, (GROUP, tokens), 0)
    position = lax.broadcasted_iota(jnp.int32, (GROUP, tokens), 1)
    begin = jnp.zeros((GROUP, tokens), jnp.int32)
    end = jnp.zeros((GROUP, tokens), jnp.int32)
    length_id = lax.broadcasted_iota(jnp.int32, (GROUP, width), 0)
    length = jnp.ones((GROUP, width), jnp.int32)
    start = jnp.int32(0)
    for r in range(requests):
        n = lens_ref[0, r]
        begin = jnp.where(row_id == r, start, begin)
        end = jnp.where(row_id == r, start + n, end)
        length = jnp.where(length_id == r, n, length)
        start = start + n
    member = jnp.where((position >= begin) & (position < end), 1.0, 0.0).astype(jnp.bfloat16)
    lat = lat_ref[...]
    logits = lax.dot_general(hid_ref[...], lat, NT, preferred_element_type=jnp.float32)
    top = jnp.max(logits, axis=1, keepdims=True)
    e = jnp.exp2((logits - top) * (math.log2(math.e) / math.sqrt(width)))
    weights = (e * (1.0 / jnp.sum(e, axis=1, keepdims=True))).astype(jnp.bfloat16)
    total = jnp.dot(member, weights, preferred_element_type=jnp.float32)
    parts = jnp.concatenate([*three_parts(total), jnp.zeros_like(total)], axis=0).astype(jnp.bfloat16)
    sums = jnp.dot(parts, lat, preferred_element_type=jnp.float32)
    sums = sums[:GROUP] + sums[GROUP : 2 * GROUP] + sums[2 * GROUP : 3 * GROUP]
    pooled = sums / length.astype(jnp.float32)
    ss_ref[...] = jnp.broadcast_to(jnp.sum(pooled * pooled, axis=1, keepdims=True), ss_ref.shape)

    for query in range(requests):
        for f in range(pieces):
            halves[query * pairs + f // 2, f % 2 : f % 2 + 1, :] = pooled[
                query : query + 1, f * LANES : (f + 1) * LANES
            ]
    rows = halves[...].astype(jnp.bfloat16)
    for place in range(pay_ref.shape[0]):
        pay_ref[place, : requests * pairs] = rows
        pay_ref[place, requests * pairs] = marks


def score_kernel(local_slots, xs, zs, requests, rows_ref, pas_ref, ss_ref, out_ref, rows, blocks):
    owners = xs * zs
    cap = LANES
    pieces = pas_ref.shape[1] // LANES
    block = rows_ref.shape[0] // owners
    bits = local_slots.bit_length() - 1
    me = (lax.axis_index(("x", "z")) * MOST).astype(jnp.float32)
    rows[...] = rows_ref[...].astype(jnp.float32)
    place = rows[pl.ds(requests * pieces, owners, stride=block), :]
    code = rows[pl.ds(requests * pieces + 1, owners, stride=block), :]
    mine = jnp.concatenate([jnp.where(place == me + float(k), code, 0.0) for k in range(MOST)], axis=0)
    ones = jnp.ones((LANES, LANES), jnp.bfloat16)
    code = jnp.dot(mine.astype(jnp.bfloat16), ones, preferred_element_type=jnp.float32).astype(jnp.int32)
    pieces_of = [
        [rows[pl.ds(q * pieces + f, owners, stride=block), :] for f in range(pieces)] for q in range(requests)
    ]
    chosen = []
    for k in range(MOST):
        query = lax.shift_right_logical(code[k * owners : (k + 1) * owners], bits)
        piece = []
        for f in range(pieces):
            got = pieces_of[0][f]
            for q in range(1, requests):
                got = jnp.where(query == q, pieces_of[q][f], got)
            piece.append(got)
        chosen.append(jnp.concatenate(piece, axis=1))
    chosen = jnp.concatenate(chosen, axis=0).astype(jnp.bfloat16)
    local = code & (local_slots - 1)
    total = jnp.zeros((MOST * owners, cap), jnp.float32)
    for s in range(0, local_slots, 2):
        got = lax.dot_general(
            chosen, pas_ref[s * cap : (s + 2) * cap, :], NT, preferred_element_type=jnp.float32
        )
        total = jnp.where(local == s, got[:, :cap], total)
        total = jnp.where(local == s + 1, got[:, cap:], total)

    tps = zs // GROUP * MOST
    part = LANES // tps
    height = out_ref.shape[0] // (xs * tps)
    lane = lax.broadcasted_iota(jnp.int32, (GROUP, LANES), 1)
    for x in range(xs):
        first = [k * owners + x * zs + h * GROUP for h in range(zs // GROUP) for k in range(MOST)]
        skew = [total[r : r + GROUP] for r in first]
        skew = [pltpu.roll(v, part * g, 1) if g else v for g, v in enumerate(skew)]
        for t in range(tps):
            mixed = skew[0]
            for g in range(1, tps):
                mixed = jnp.where(lane // part == (t + g) % tps, skew[g], mixed)
            mixed = pltpu.roll(mixed, LANES - part * t, 1) if t else mixed
            row = (x * tps + t) * height
            blocks[row : row + GROUP, :] = mixed
    lane = lax.broadcasted_iota(jnp.int32, (1, LANES), 1)
    squares = ss_ref[0:1, :]
    for q in range(1, requests):
        squares = jnp.where(lane % (LANES // 2) // part == q, ss_ref[q : q + 1, :], squares)
    hi, mid, low = three_parts(squares)
    parts = jnp.concatenate([jnp.where(lane < LANES // 2, hi, mid), low], axis=0)
    for i in range(xs * tps):
        blocks[i * height + GROUP : (i + 1) * height, :] = parts
    out_ref[...] = blocks[...].astype(jnp.bfloat16)


def merge_kernel(xs, tps, got_ref, out_ref, ss_ref, blocks):
    height = blocks.shape[0] // (xs * tps)
    blocks[...] = got_ref[...].astype(jnp.float32)
    total = []
    for x in range(xs):
        acc = blocks[x * tps * height : x * tps * height + GROUP, :]
        for t in range(1, tps):
            row = (x * tps + t) * height
            acc = acc + blocks[row : row + GROUP, :]
        total.append(acc)
    left = lax.broadcasted_iota(jnp.int32, (GROUP, LANES), 1) < LANES // 2
    halves = xs // 2
    for r in range(halves):
        one, two = total[2 * r], total[2 * r + 1]
        near = jnp.where(left, one, pltpu.roll(two, LANES // 2, 1))
        far = jnp.where(left, pltpu.roll(one, LANES // 2, 1), two)
        out_ref[pl.ds(r, GROUP, stride=halves), :] = near
        out_ref[pl.ds(GROUP * halves + r, GROUP, stride=halves), :] = far
    mine = lax.axis_index("x") * (tps * height) + GROUP
    top = blocks[pl.ds(mine, 1), :]
    low = blocks[pl.ds(mine + 1, 1), :]
    for t in range(1, tps):
        top = top + blocks[pl.ds(mine + t * height, 1), :]
        low = low + blocks[pl.ds(mine + t * height + 1, 1), :]
    ss_ref[...] = jnp.broadcast_to(top + pltpu.roll(top, LANES // 2, 1) + low, ss_ref.shape)


def finish_kernel(sel_ref, got_ref, ss_ref, out_ref):
    requests, nprobe, part = out_ref.shape
    height = got_ref.shape[0]
    one_hot = sel_ref[:, :height].astype(jnp.bfloat16)
    parts = jnp.concatenate(three_parts(got_ref[...]), axis=1).astype(jnp.bfloat16)
    rows = jnp.dot(one_hot, parts, preferred_element_type=jnp.float32)
    rows = rows[:, :LANES] + rows[:, LANES : 2 * LANES] + rows[:, 2 * LANES :]
    rows = jnp.where(sel_ref[:, LANES:] > 0.0, rows, 0.0)
    step = LANES // 2
    while step >= part:
        rows = rows + pltpu.roll(rows, step, 1)
        step //= 2
    norm = jnp.sqrt(ss_ref[...] + 1e-06)
    for q in range(requests):
        here = pltpu.roll(norm, LANES - part * q, 1) if q else norm
        out_ref[q] = (rows[q * nprobe : (q + 1) * nprobe, :] / here)[:, :part]


def pool(local_slots, xs, zs, tps, lengths, probes, cluster_slot, slab_sizes, hidden, latents):
    pairs = hidden.shape[1] // LANES // 2
    whole = jnp.int32
    operands = (lengths, probes, cluster_slot, slab_sizes, hidden, latents)
    return pl.pallas_call(
        functools.partial(pool_kernel, local_slots, xs, zs, tps),
        out_shape=(
            jax.ShapeDtypeStruct((zs, probes.shape[0] * pairs + 1, 2, LANES), jnp.bfloat16),
            jax.ShapeDtypeStruct((GROUP, LANES), jnp.float32),
            jax.ShapeDtypeStruct((probes.size, 2 * LANES), jnp.float32),
        ),
        in_specs=[HBM] * len(operands),
        out_specs=(VMEM, VMEM, VMEM),
        scratch_shapes=[
            pltpu.VMEM((probes.shape[0] * pairs, 2, LANES), jnp.float32),
            pltpu.SMEM((xs * zs,), whole),
            pltpu.SMEM(lengths.shape, whole),
            pltpu.SMEM(probes.shape, whole),
            pltpu.SMEM(cluster_slot.shape, whole),
            pltpu.SMEM(slab_sizes.shape, whole),
            pltpu.VMEM(hidden.shape, hidden.dtype),
            pltpu.VMEM(latents.shape, latents.dtype),
            pltpu.SemaphoreType.DMA((len(operands),)),
        ],
        name="pool",
        compiler_params=PARAMS,
    )(*(pltpu.with_memory_space_constraint(x, pltpu.HBM) for x in operands))


def score(xs, zs, tps, requests, rows, passages, squares):
    local_slots, cap, width = passages.shape
    blocks = (xs * tps * (GROUP + 2), LANES)
    return pl.pallas_call(
        functools.partial(score_kernel, local_slots, xs, zs, requests),
        out_shape=jax.ShapeDtypeStruct(blocks, jnp.bfloat16),
        in_specs=[VMEM, VMEM, VMEM],
        out_specs=VMEM,
        scratch_shapes=[pltpu.VMEM(rows.shape, jnp.float32), pltpu.VMEM(blocks, jnp.float32)],
        name="score",
        compiler_params=PARAMS,
    )(rows, passages.reshape(local_slots * cap, width), squares)


def merge(xs, zs, tps, got):
    return pl.pallas_call(
        functools.partial(merge_kernel, xs, tps),
        out_shape=(
            jax.ShapeDtypeStruct((zs * xs // 2, LANES), jnp.float32),
            jax.ShapeDtypeStruct((GROUP, LANES), jnp.float32),
        ),
        in_specs=[VMEM],
        out_specs=(VMEM, VMEM),
        scratch_shapes=[pltpu.VMEM(got.shape, jnp.float32)],
        name="merge",
        compiler_params=PARAMS,
    )(got)


def finish(requests, nprobe, part, select, got, squares):
    return pl.pallas_call(
        finish_kernel,
        out_shape=jax.ShapeDtypeStruct((requests, nprobe, part), jnp.float32),
        in_specs=[VMEM, VMEM, VMEM],
        out_specs=VMEM,
        name="finish",
        compiler_params=PARAMS,
    )(select, got, squares)


def per_device(xs, zs, tps, hidden, latents, lengths, probes, cluster_slot, slab_sizes, passages):
    local_slots, cap, _ = passages.shape
    requests, nprobe = probes.shape
    payload, squares, select = pool(
        local_slots, xs, zs, tps, lengths, probes, cluster_slot, slab_sizes, hidden, latents
    )
    blocks = lax.all_to_all(payload, "z", 0, 0, tiled=True)
    blocks = jnp.broadcast_to(blocks[None], (xs, *blocks.shape))
    rows = lax.all_to_all(blocks, "x", 0, 0, tiled=True).reshape(-1, LANES)
    partial = score(xs, zs, tps, requests, rows, passages, squares)
    blocks = lax.all_to_all(partial.reshape(xs * tps, -1, 2, LANES), ("x", "tp"), 0, 0, tiled=True)
    columns, squares = merge(xs, zs, tps, blocks.reshape(partial.shape))
    got = lax.all_to_all(columns.reshape(zs, 1, -1), "z", 0, 0, tiled=True)
    return finish(requests, nprobe, cap // tps, select, got.reshape(columns.shape), squares)


def solution(mesh):
    tps = mesh.shape["tp"]
    zs = mesh.shape["shard"] // XS
    fine = Mesh(mesh.devices.reshape(XS, zs, tps), ("x", "z", "tp"))
    shard = ("x", "z")
    placed = (
        P(shard, "tp"),
        P(None, "tp"),
        P(shard, None),
        P(shard, None),
        P(),
        P(),
        P(shard, None, "tp"),
    )
    return jax.shard_map(
        functools.partial(per_device, XS, zs, tps),
        mesh=fine,
        in_specs=placed,
        out_specs=P(shard, None, "tp"),
        check_vma=False,
    )
```

```python
import functools
import math

import jax
import jax.numpy as jnp
from jax import lax
from jax.experimental import pallas as pl
from jax.experimental.pallas import tpu as pltpu
from jax.sharding import Mesh
from jax.sharding import PartitionSpec as P

MOST = 4
LANES = 128
GROUP = 8
XS = 4
VMEM = pl.BlockSpec(memory_space=pltpu.VMEM)
HBM = pl.BlockSpec(memory_space=pltpu.HBM)
NT = (((1,), (1,)), ((), ()))
PARAMS = pltpu.CompilerParams(vmem_limit_bytes=16 << 20)


def three_parts(value):
    hi = value.astype(jnp.bfloat16).astype(jnp.float32)
    rest = value - hi
    mid = rest.astype(jnp.bfloat16).astype(jnp.float32)
    return hi, mid, rest - mid


def pool_kernel(
    local_slots, xs, zs, tps, lens_hbm, probes_hbm, slot_hbm, size_hbm, hid_hbm, lat_hbm,
    pay_ref, ss_ref, sel_ref,
    halves, count, lens_ref, probes_ref, slot_ref, size_ref, hid_ref, lat_ref, sems,
):
    tokens, width = hid_ref.shape
    requests, nprobe = probes_ref.shape
    pieces = width // LANES
    pairs = pieces // 2
    bits = local_slots.bit_length() - 1
    copies = [
        pltpu.make_async_copy(source, target, sems.at[i])
        for i, (source, target) in enumerate(
            [
                (probes_hbm, probes_ref),
                (slot_hbm, slot_ref),
                (lens_hbm, lens_ref),
                (size_hbm, size_ref),
                (lat_hbm, lat_ref),
                (hid_hbm, hid_ref),
            ]
        )
    ]
    for copy in copies:
        copy.start()
    for owner in range(xs * zs):
        count[owner] = 0
    for copy in copies[:4]:
        copy.wait()

    spot = lax.broadcasted_iota(jnp.int32, (1, LANES), 1)
    part = LANES // tps
    column = (spot & (part - 1)) + lax.axis_index("tp") * part
    group_of = lax.shift_right_logical(spot, part.bit_length() - 1)
    lane = lax.broadcasted_iota(jnp.int32, (2, LANES), 1)
    first = lax.broadcasted_iota(jnp.int32, (2, LANES), 0) == 0
    marks = jnp.full((2, LANES), -1, jnp.int32)
    for query in range(requests):
        for j in range(nprobe):
            item = query * nprobe + j
            cluster = probes_ref[query, j]
            slot = slot_ref[cluster]
            owner = lax.shift_right_logical(slot, bits)
            rank = jnp.minimum(count[owner], MOST - 1)
            count[owner] = rank + 1
            place = owner * MOST + rank
            x, z = lax.shift_right_logical(owner, zs.bit_length() - 1), owner & (zs - 1)
            row = z * (xs // 2) + lax.shift_right_logical(x, 1)
            here = (group_of == (x & 1) * MOST + rank) & (column < size_ref[cluster])
            sel_ref[item : item + 1, :LANES] = jnp.where(spot == row, 1.0, 0.0)
            sel_ref[item : item + 1, LANES:] = jnp.where(here, 1.0, 0.0)
            code = (query << bits) + (slot & (local_slots - 1))
            marks = jnp.where(lane == item, jnp.where(first, place, code), marks)
    marks = marks.astype(jnp.float32).astype(jnp.bfloat16)
    for copy in copies[4:]:
        copy.wait()

    row_id = lax.broadcasted_iota(jnp.int32, (GROUP, tokens), 0)
    position = lax.broadcasted_iota(jnp.int32, (GROUP, tokens), 1)
    begin = jnp.zeros((GROUP, tokens), jnp.int32)
    end = jnp.zeros((GROUP, tokens), jnp.int32)
    length_id = lax.broadcasted_iota(jnp.int32, (GROUP, width), 0)
    length = jnp.ones((GROUP, width), jnp.int32)
    start = jnp.int32(0)
    for r in range(requests):
        n = lens_ref[0, r]
        begin = jnp.where(row_id == r, start, begin)
        end = jnp.where(row_id == r, start + n, end)
        length = jnp.where(length_id == r, n, length)
        start = start + n
    member = jnp.where((position >= begin) & (position < end), 1.0, 0.0).astype(jnp.bfloat16)
    lat = lat_ref[...]
    logits = lax.dot_general(hid_ref[...], lat, NT, preferred_element_type=jnp.float32)
    top = jnp.max(logits, axis=1, keepdims=True)
    e = jnp.exp2((logits - top) * (math.log2(math.e) / math.sqrt(width)))
    weights = (e * (1.0 / jnp.sum(e, axis=1, keepdims=True))).astype(jnp.bfloat16)
    total = jnp.dot(member, weights, preferred_element_type=jnp.float32)
    parts = jnp.concatenate([*three_parts(total), jnp.zeros_like(total)], axis=0).astype(jnp.bfloat16)
    sums = jnp.dot(parts, lat, preferred_element_type=jnp.float32)
    sums = sums[:GROUP] + sums[GROUP : 2 * GROUP] + sums[2 * GROUP : 3 * GROUP]
    pooled = sums / length.astype(jnp.float32)
    ss_ref[...] = jnp.broadcast_to(jnp.sum(pooled * pooled, axis=1, keepdims=True), ss_ref.shape)

    for query in range(requests):
        for f in range(pieces):
            halves[query * pairs + f // 2, f % 2 : f % 2 + 1, :] = pooled[
                query : query + 1, f * LANES : (f + 1) * LANES
            ]
    rows = halves[...].astype(jnp.bfloat16)
    for place in range(pay_ref.shape[0]):
        pay_ref[place, : requests * pairs] = rows
        pay_ref[place, requests * pairs] = marks


def score_kernel(local_slots, xs, zs, requests, rows_ref, pas_ref, ss_ref, out_ref, rows, blocks):
    owners = xs * zs
    cap = LANES
    pieces = pas_ref.shape[1] // LANES
    block = rows_ref.shape[0] // owners
    bits = local_slots.bit_length() - 1
    me = (lax.axis_index(("x", "z")) * MOST).astype(jnp.float32)
    rows[: rows_ref.shape[0], :] = rows_ref[...].astype(jnp.float32)
    place = rows[pl.ds(requests * pieces, owners, stride=block), :]
    code = rows[pl.ds(requests * pieces + 1, owners, stride=block), :]
    mine = jnp.concatenate([jnp.where(place == me + float(k), code, 0.0) for k in range(MOST)], axis=0)
    ones = jnp.ones((LANES, LANES), jnp.bfloat16)
    code = jnp.dot(mine.astype(jnp.bfloat16), ones, preferred_element_type=jnp.float32).astype(jnp.int32)
    pieces_of = [
        [rows[pl.ds(q * pieces + f, owners, stride=block), :] for f in range(pieces)] for q in range(requests)
    ]
    chosen = []
    for k in range(MOST):
        query = lax.shift_right_logical(code[k * owners : (k + 1) * owners], bits)
        piece = []
        for f in range(pieces):
            got = pieces_of[0][f]
            for q in range(1, requests):
                got = jnp.where(query == q, pieces_of[q][f], got)
            piece.append(got)
        chosen.append(jnp.concatenate(piece, axis=1))
    chosen = jnp.concatenate(chosen, axis=0).astype(jnp.bfloat16)
    local = code & (local_slots - 1)
    total = jnp.zeros((MOST * owners, cap), jnp.float32)
    for s in range(0, local_slots, 2):
        got = lax.dot_general(
            chosen, pas_ref[s * cap : (s + 2) * cap, :], NT, preferred_element_type=jnp.float32
        )
        total = jnp.where(local == s, got[:, :cap], total)
        total = jnp.where(local == s + 1, got[:, cap:], total)

    tps = zs // GROUP * MOST
    part = LANES // tps
    height = out_ref.shape[0] // (xs * tps)
    lane = lax.broadcasted_iota(jnp.int32, (GROUP, LANES), 1)
    for x in range(xs):
        first = [k * owners + x * zs + h * GROUP for h in range(zs // GROUP) for k in range(MOST)]
        skew = [total[r : r + GROUP] for r in first]
        skew = [pltpu.roll(v, part * g, 1) if g else v for g, v in enumerate(skew)]
        for t in range(tps):
            mixed = skew[0]
            for g in range(1, tps):
                mixed = jnp.where(lane // part == (t + g) % tps, skew[g], mixed)
            mixed = pltpu.roll(mixed, LANES - part * t, 1) if t else mixed
            row = (x * tps + t) * height
            blocks[row : row + GROUP, :] = mixed
    lane = lax.broadcasted_iota(jnp.int32, (1, LANES), 1)
    squares = ss_ref[0:1, :]
    for q in range(1, requests):
        squares = jnp.where(lane % (LANES // 2) // part == q, ss_ref[q : q + 1, :], squares)
    hi, mid, low = three_parts(squares)
    parts = jnp.concatenate([jnp.where(lane < LANES // 2, hi, mid), low], axis=0)
    for i in range(xs * tps):
        blocks[i * height + GROUP : (i + 1) * height, :] = parts
    out_ref[...] = blocks[...].astype(jnp.bfloat16)


def merge_kernel(xs, tps, got_ref, out_ref, ss_ref, blocks, columns):
    height = got_ref.shape[0] // (xs * tps)
    blocks[: got_ref.shape[0], :] = got_ref[...].astype(jnp.float32)
    total = []
    for x in range(xs):
        acc = blocks[x * tps * height : x * tps * height + GROUP, :]
        for t in range(1, tps):
            row = (x * tps + t) * height
            acc = acc + blocks[row : row + GROUP, :]
        total.append(acc)
    left = lax.broadcasted_iota(jnp.int32, (GROUP, LANES), 1) < LANES // 2
    halves = xs // 2
    for r in range(halves):
        one, two = total[2 * r], total[2 * r + 1]
        near = jnp.where(left, one, pltpu.roll(two, LANES // 2, 1))
        far = jnp.where(left, pltpu.roll(one, LANES // 2, 1), two)
        columns[pl.ds(r, GROUP, stride=halves), :] = near
        columns[pl.ds(GROUP * halves + r, GROUP, stride=halves), :] = far
    out_ref[...] = columns[: out_ref.shape[0], :]
    mine = lax.axis_index("x") * (tps * height) + GROUP
    top = blocks[pl.ds(mine, 1), :]
    low = blocks[pl.ds(mine + 1, 1), :]
    for t in range(1, tps):
        top = top + blocks[pl.ds(mine + t * height, 1), :]
        low = low + blocks[pl.ds(mine + t * height + 1, 1), :]
    ss_ref[...] = jnp.broadcast_to(top + pltpu.roll(top, LANES // 2, 1) + low, ss_ref.shape)


def finish_kernel(sel_ref, got_ref, ss_ref, out_ref):
    requests, nprobe, part = out_ref.shape
    height = got_ref.shape[0]
    one_hot = sel_ref[:, :height].astype(jnp.bfloat16)
    parts = jnp.concatenate(three_parts(got_ref[...]), axis=1).astype(jnp.bfloat16)
    rows = jnp.dot(one_hot, parts, preferred_element_type=jnp.float32)
    rows = rows[:, :LANES] + rows[:, LANES : 2 * LANES] + rows[:, 2 * LANES :]
    rows = jnp.where(sel_ref[:, LANES:] > 0.0, rows, 0.0)
    step = LANES // 2
    while step >= part:
        rows = rows + pltpu.roll(rows, step, 1)
        step //= 2
    norm = jnp.sqrt(ss_ref[...] + 1e-06)
    for q in range(requests):
        here = pltpu.roll(norm, LANES - part * q, 1) if q else norm
        out_ref[q] = (rows[q * nprobe : (q + 1) * nprobe, :] / here)[:, :part]


def pool(local_slots, xs, zs, tps, lengths, probes, cluster_slot, slab_sizes, hidden, latents):
    pairs = hidden.shape[1] // LANES // 2
    whole = jnp.int32
    operands = (lengths, probes, cluster_slot, slab_sizes, hidden, latents)
    return pl.pallas_call(
        functools.partial(pool_kernel, local_slots, xs, zs, tps),
        out_shape=(
            jax.ShapeDtypeStruct((zs, probes.shape[0] * pairs + 1, 2, LANES), jnp.bfloat16),
            jax.ShapeDtypeStruct((GROUP, LANES), jnp.float32),
            jax.ShapeDtypeStruct((probes.size, 2 * LANES), jnp.float32),
        ),
        in_specs=[HBM] * len(operands),
        out_specs=(VMEM, VMEM, VMEM),
        scratch_shapes=[
            pltpu.VMEM((probes.shape[0] * pairs, 2, LANES), jnp.float32),
            pltpu.SMEM((xs * zs,), whole),
            pltpu.SMEM(lengths.shape, whole),
            pltpu.SMEM(probes.shape, whole),
            pltpu.SMEM(cluster_slot.shape, whole),
            pltpu.SMEM(slab_sizes.shape, whole),
            pltpu.VMEM(hidden.shape, hidden.dtype),
            pltpu.VMEM(latents.shape, latents.dtype),
            pltpu.SemaphoreType.DMA((len(operands),)),
        ],
        name="pool",
        compiler_params=PARAMS,
    )(*(pltpu.with_memory_space_constraint(x, pltpu.HBM) for x in operands))


def score(xs, zs, tps, requests, rows, passages, squares):
    local_slots, cap, width = passages.shape
    blocks = (xs * tps * (GROUP + 2), LANES)
    return pl.pallas_call(
        functools.partial(score_kernel, local_slots, xs, zs, requests),
        out_shape=jax.ShapeDtypeStruct(blocks, jnp.bfloat16),
        in_specs=[VMEM, VMEM, VMEM],
        out_specs=VMEM,
        scratch_shapes=[
            pltpu.VMEM((rows.shape[0] + 3 * GROUP, LANES), jnp.float32),
            pltpu.VMEM(blocks, jnp.float32),
        ],
        name="score",
        compiler_params=PARAMS,
    )(rows, passages.reshape(local_slots * cap, width), squares)


def merge(xs, zs, tps, got):
    return pl.pallas_call(
        functools.partial(merge_kernel, xs, tps),
        out_shape=(
            jax.ShapeDtypeStruct((zs * xs // 2, LANES), jnp.float32),
            jax.ShapeDtypeStruct((GROUP, LANES), jnp.float32),
        ),
        in_specs=[VMEM],
        out_specs=(VMEM, VMEM),
        scratch_shapes=[
            pltpu.VMEM((got.shape[0] + GROUP, LANES), jnp.float32),
            pltpu.VMEM((zs * xs // 2 + GROUP, LANES), jnp.float32),
        ],
        name="merge",
        compiler_params=PARAMS,
    )(got)


def finish(requests, nprobe, part, select, got, squares):
    return pl.pallas_call(
        finish_kernel,
        out_shape=jax.ShapeDtypeStruct((requests, nprobe, part), jnp.float32),
        in_specs=[VMEM, VMEM, VMEM],
        out_specs=VMEM,
        name="finish",
        compiler_params=PARAMS,
    )(select, got, squares)


def per_device(xs, zs, tps, hidden, latents, lengths, probes, cluster_slot, slab_sizes, passages):
    local_slots, cap, _ = passages.shape
    requests, nprobe = probes.shape
    payload, squares, select = pool(
        local_slots, xs, zs, tps, lengths, probes, cluster_slot, slab_sizes, hidden, latents
    )
    blocks = lax.all_to_all(payload, "z", 0, 0, tiled=True)
    blocks = jnp.broadcast_to(blocks[None], (xs, *blocks.shape))
    rows = lax.all_to_all(blocks, "x", 0, 0, tiled=True).reshape(-1, LANES)
    partial = score(xs, zs, tps, requests, rows, passages, squares)
    blocks = lax.all_to_all(partial.reshape(xs * tps, -1, 2, LANES), ("x", "tp"), 0, 0, tiled=True)
    columns, squares = merge(xs, zs, tps, blocks.reshape(partial.shape))
    got = lax.all_to_all(columns.reshape(zs, 1, -1), "z", 0, 0, tiled=True)
    return finish(requests, nprobe, cap // tps, select, got.reshape(columns.shape), squares)


def solution(mesh):
    tps = mesh.shape["tp"]
    zs = mesh.shape["shard"] // XS
    fine = Mesh(mesh.devices.reshape(XS, zs, tps), ("x", "z", "tp"))
    shard = ("x", "z")
    placed = (
        P(shard, "tp"),
        P(None, "tp"),
        P(shard, None),
        P(shard, None),
        P(),
        P(),
        P(shard, None, "tp"),
    )
    return jax.shard_map(
        functools.partial(per_device, XS, zs, tps),
        mesh=fine,
        in_specs=placed,
        out_specs=P(shard, None, "tp"),
        check_vma=False,
    )
```

```python
import functools
import math

import jax
import jax.numpy as jnp
from jax import lax
from jax.experimental import pallas as pl
from jax.experimental.pallas import tpu as pltpu
from jax.sharding import Mesh
from jax.sharding import PartitionSpec as P

MOST = 4
LANES = 128
GROUP = 8
XS = 4
PACK_ROWS = 18
VMEM = pl.BlockSpec(memory_space=pltpu.VMEM)
HBM = pl.BlockSpec(memory_space=pltpu.HBM)
NT = (((1,), (1,)), ((), ()))
PARAMS = pltpu.CompilerParams(vmem_limit_bytes=16 << 20)


def three_parts(value):
    hi = value.astype(jnp.bfloat16).astype(jnp.float32)
    rest = value - hi
    mid = rest.astype(jnp.bfloat16).astype(jnp.float32)
    return hi, mid, rest - mid


def pool_kernel(
    local_slots, xs, zs, tps, lens_hbm, probes_hbm, slot_hbm, size_hbm, hid_hbm, lat_hbm,
    pay_ref, ss_ref, sel_ref,
    halves, count, lens_ref, probes_ref, slot_ref, size_ref, hid_ref, lat_ref, sems,
):
    tokens, width = hid_ref.shape
    requests, nprobe = probes_ref.shape
    pieces = width // LANES
    pairs = pieces // 2
    bits = local_slots.bit_length() - 1
    copies = [
        pltpu.make_async_copy(source, target, sems.at[i])
        for i, (source, target) in enumerate(
            [
                (probes_hbm, probes_ref),
                (slot_hbm, slot_ref),
                (lens_hbm, lens_ref),
                (size_hbm, size_ref),
                (lat_hbm, lat_ref),
                (hid_hbm, hid_ref),
            ]
        )
    ]
    for copy in copies:
        copy.start()
    for owner in range(xs * zs):
        count[owner] = 0
    for copy in copies[:4]:
        copy.wait()

    spot = lax.broadcasted_iota(jnp.int32, (1, LANES), 1)
    part = LANES // tps
    column = (spot & (part - 1)) + lax.axis_index("tp") * part
    group_of = lax.shift_right_logical(spot, part.bit_length() - 1)
    items = requests * nprobe
    lane = lax.broadcasted_iota(jnp.int32, (2, LANES), 1)
    marks = jnp.full((2, LANES), -1, jnp.int32)
    for query in range(requests):
        for j in range(nprobe):
            item = query * nprobe + j
            cluster = probes_ref[query, j]
            slot = slot_ref[cluster]
            owner = lax.shift_right_logical(slot, bits)
            rank = jnp.minimum(count[owner], MOST - 1)
            count[owner] = rank + 1
            place = owner * MOST + rank
            x, z = lax.shift_right_logical(owner, zs.bit_length() - 1), owner & (zs - 1)
            row = z * (xs // 2) + lax.shift_right_logical(x, 1)
            here = (group_of == (x & 1) * MOST + rank) & (column < size_ref[cluster])
            sel_ref[item : item + 1, :LANES] = jnp.where(spot == row, 1.0, 0.0)
            sel_ref[item : item + 1, LANES:] = jnp.where(here, 1.0, 0.0)
            code = (query << bits) + (slot & (local_slots - 1))
            marks = jnp.where(lane == item, place, jnp.where(lane == items + item, code, marks))
    marks = marks.astype(jnp.float32).astype(jnp.bfloat16)
    for copy in copies[4:]:
        copy.wait()

    row_id = lax.broadcasted_iota(jnp.int32, (GROUP, tokens), 0)
    position = lax.broadcasted_iota(jnp.int32, (GROUP, tokens), 1)
    begin = jnp.zeros((GROUP, tokens), jnp.int32)
    end = jnp.zeros((GROUP, tokens), jnp.int32)
    length_id = lax.broadcasted_iota(jnp.int32, (GROUP, width), 0)
    length = jnp.ones((GROUP, width), jnp.int32)
    start = jnp.int32(0)
    for r in range(requests):
        n = lens_ref[0, r]
        begin = jnp.where(row_id == r, start, begin)
        end = jnp.where(row_id == r, start + n, end)
        length = jnp.where(length_id == r, n, length)
        start = start + n
    member = jnp.where((position >= begin) & (position < end), 1.0, 0.0).astype(jnp.bfloat16)
    lat = lat_ref[...]
    logits = lax.dot_general(hid_ref[...], lat, NT, preferred_element_type=jnp.float32)
    top = jnp.max(logits, axis=1, keepdims=True)
    e = jnp.exp2((logits - top) * (math.log2(math.e) / math.sqrt(width)))
    weights = (e * (1.0 / jnp.sum(e, axis=1, keepdims=True))).astype(jnp.bfloat16)
    total = jnp.dot(member, weights, preferred_element_type=jnp.float32)
    parts = jnp.concatenate([*three_parts(total), jnp.zeros_like(total)], axis=0).astype(jnp.bfloat16)
    sums = jnp.dot(parts, lat, preferred_element_type=jnp.float32)
    sums = sums[:GROUP] + sums[GROUP : 2 * GROUP] + sums[2 * GROUP : 3 * GROUP]
    pooled = sums / length.astype(jnp.float32)
    ss_ref[...] = jnp.broadcast_to(jnp.sum(pooled * pooled, axis=1, keepdims=True), ss_ref.shape)

    for query in range(requests):
        for f in range(pieces):
            halves[query * pairs + f // 2, f % 2 : f % 2 + 1, :] = pooled[
                query : query + 1, f * LANES : (f + 1) * LANES
            ]
    rows = halves[...].astype(jnp.bfloat16)
    for place in range(pay_ref.shape[0]):
        pay_ref[place, : requests * pairs] = rows
        pay_ref[place, requests * pairs] = marks


def spread_kernel(got_ref, out_ref, rows):
    copies = out_ref.shape[0]
    packs = got_ref.shape[0] // PACK_ROWS
    rows[: got_ref.shape[0], :] = got_ref[...].astype(jnp.float32)
    pieces = [rows[pl.ds(i, packs, stride=PACK_ROWS), :] for i in range(PACK_ROWS - 1)]
    block = jnp.concatenate(pieces, axis=0).astype(jnp.bfloat16)
    for x in range(copies):
        out_ref[x] = block


def score_kernel(local_slots, xs, zs, requests, items, rows_ref, pas_ref, ss_ref, out_ref, blocks):
    owners = xs * zs
    cap = LANES
    pieces = pas_ref.shape[1] // LANES
    bits = local_slots.bit_length() - 1
    me = (lax.axis_index(("x", "z")) * MOST).astype(jnp.float32)

    def piece_of(i):
        starts = [x * (rows_ref.shape[0] // xs) + i * zs for x in range(xs)]
        return jnp.concatenate([rows_ref[r : r + zs, :] for r in starts], axis=0).astype(jnp.float32)

    marks = piece_of(requests * pieces)
    lane = lax.broadcasted_iota(jnp.int32, marks.shape, 1)
    place = jnp.where(lane < items, marks, -1.0)
    code = pltpu.roll(marks, LANES - items, 1)
    mine = jnp.concatenate([jnp.where(place == me + float(k), code, 0.0) for k in range(MOST)], axis=0)
    ones = jnp.ones((LANES, LANES), jnp.bfloat16)
    code = jnp.dot(mine.astype(jnp.bfloat16), ones, preferred_element_type=jnp.float32).astype(jnp.int32)
    pieces_of = [[piece_of(q * pieces + f) for f in range(pieces)] for q in range(requests)]
    chosen = []
    for k in range(MOST):
        query = lax.shift_right_logical(code[k * owners : (k + 1) * owners], bits)
        piece = []
        for f in range(pieces):
            got = pieces_of[0][f]
            for q in range(1, requests):
                got = jnp.where(query == q, pieces_of[q][f], got)
            piece.append(got)
        chosen.append(jnp.concatenate(piece, axis=1))
    chosen = jnp.concatenate(chosen, axis=0).astype(jnp.bfloat16)
    local = code & (local_slots - 1)
    total = jnp.zeros((MOST * owners, cap), jnp.float32)
    for s in range(0, local_slots, 2):
        got = lax.dot_general(
            chosen, pas_ref[s * cap : (s + 2) * cap, :], NT, preferred_element_type=jnp.float32
        )
        total = jnp.where(local == s, got[:, :cap], total)
        total = jnp.where(local == s + 1, got[:, cap:], total)

    tps = zs // GROUP * MOST
    part = LANES // tps
    height = out_ref.shape[0] // (xs * tps)
    lane = lax.broadcasted_iota(jnp.int32, (GROUP, LANES), 1)
    for x in range(xs):
        first = [k * owners + x * zs + h * GROUP for h in range(zs // GROUP) for k in range(MOST)]
        skew = [total[r : r + GROUP] for r in first]
        skew = [pltpu.roll(v, part * g, 1) if g else v for g, v in enumerate(skew)]
        for t in range(tps):
            mixed = skew[0]
            for g in range(1, tps):
                mixed = jnp.where(lane // part == (t + g) % tps, skew[g], mixed)
            mixed = pltpu.roll(mixed, LANES - part * t, 1) if t else mixed
            row = (x * tps + t) * height
            blocks[row : row + GROUP, :] = mixed
    lane = lax.broadcasted_iota(jnp.int32, (1, LANES), 1)
    squares = ss_ref[0:1, :]
    for q in range(1, requests):
        squares = jnp.where(lane % (LANES // 2) // part == q, ss_ref[q : q + 1, :], squares)
    hi, mid, low = three_parts(squares)
    parts = jnp.concatenate([jnp.where(lane < LANES // 2, hi, mid), low], axis=0)
    for i in range(xs * tps):
        blocks[i * height + GROUP : (i + 1) * height, :] = parts
    out_ref[...] = blocks[...].astype(jnp.bfloat16)


def merge_kernel(xs, tps, got_ref, out_ref, ss_ref, blocks, columns):
    height = got_ref.shape[0] // (xs * tps)
    blocks[: got_ref.shape[0], :] = got_ref[...].astype(jnp.float32)
    total = []
    for x in range(xs):
        acc = blocks[x * tps * height : x * tps * height + GROUP, :]
        for t in range(1, tps):
            row = (x * tps + t) * height
            acc = acc + blocks[row : row + GROUP, :]
        total.append(acc)
    left = lax.broadcasted_iota(jnp.int32, (GROUP, LANES), 1) < LANES // 2
    halves = xs // 2
    for r in range(halves):
        one, two = total[2 * r], total[2 * r + 1]
        near = jnp.where(left, one, pltpu.roll(two, LANES // 2, 1))
        far = jnp.where(left, pltpu.roll(one, LANES // 2, 1), two)
        columns[pl.ds(r, GROUP, stride=halves), :] = near
        columns[pl.ds(GROUP * halves + r, GROUP, stride=halves), :] = far
    out_ref[...] = columns[: out_ref.shape[0], :]
    mine = lax.axis_index("x") * (tps * height) + GROUP
    top = blocks[pl.ds(mine, 1), :]
    low = blocks[pl.ds(mine + 1, 1), :]
    for t in range(1, tps):
        top = top + blocks[pl.ds(mine + t * height, 1), :]
        low = low + blocks[pl.ds(mine + t * height + 1, 1), :]
    ss_ref[...] = jnp.broadcast_to(top + pltpu.roll(top, LANES // 2, 1) + low, ss_ref.shape)


def finish_kernel(sel_ref, got_ref, ss_ref, out_ref):
    requests, nprobe, part = out_ref.shape
    height = got_ref.shape[0]
    one_hot = sel_ref[:, :height].astype(jnp.bfloat16)
    parts = jnp.concatenate(three_parts(got_ref[...]), axis=1).astype(jnp.bfloat16)
    rows = jnp.dot(one_hot, parts, preferred_element_type=jnp.float32)
    rows = rows[:, :LANES] + rows[:, LANES : 2 * LANES] + rows[:, 2 * LANES :]
    rows = jnp.where(sel_ref[:, LANES:] > 0.0, rows, 0.0)
    step = LANES // 2
    while step >= part:
        rows = rows + pltpu.roll(rows, step, 1)
        step //= 2
    norm = jnp.sqrt(ss_ref[...] + 1e-06)
    for q in range(requests):
        here = pltpu.roll(norm, LANES - part * q, 1) if q else norm
        out_ref[q] = (rows[q * nprobe : (q + 1) * nprobe, :] / here)[:, :part]


def pool(local_slots, xs, zs, tps, lengths, probes, cluster_slot, slab_sizes, hidden, latents):
    pairs = hidden.shape[1] // LANES // 2
    whole = jnp.int32
    operands = (lengths, probes, cluster_slot, slab_sizes, hidden, latents)
    return pl.pallas_call(
        functools.partial(pool_kernel, local_slots, xs, zs, tps),
        out_shape=(
            jax.ShapeDtypeStruct((zs, probes.shape[0] * pairs + 1, 2, LANES), jnp.bfloat16),
            jax.ShapeDtypeStruct((GROUP, LANES), jnp.float32),
            jax.ShapeDtypeStruct((probes.size, 2 * LANES), jnp.float32),
        ),
        in_specs=[HBM] * len(operands),
        out_specs=(VMEM, VMEM, VMEM),
        scratch_shapes=[
            pltpu.VMEM((probes.shape[0] * pairs, 2, LANES), jnp.float32),
            pltpu.SMEM((xs * zs,), whole),
            pltpu.SMEM(lengths.shape, whole),
            pltpu.SMEM(probes.shape, whole),
            pltpu.SMEM(cluster_slot.shape, whole),
            pltpu.SMEM(slab_sizes.shape, whole),
            pltpu.VMEM(hidden.shape, hidden.dtype),
            pltpu.VMEM(latents.shape, latents.dtype),
            pltpu.SemaphoreType.DMA((len(operands),)),
        ],
        name="pool",
        compiler_params=PARAMS,
    )(*(pltpu.with_memory_space_constraint(x, pltpu.HBM) for x in operands))


def spread(xs, zs, got):
    return pl.pallas_call(
        spread_kernel,
        out_shape=jax.ShapeDtypeStruct((xs, zs * (PACK_ROWS - 1), LANES), jnp.bfloat16),
        in_specs=[VMEM],
        out_specs=VMEM,
        scratch_shapes=[pltpu.VMEM((got.shape[0] + 3 * GROUP, LANES), jnp.float32)],
        name="spread",
        compiler_params=PARAMS,
    )(got)


def score(xs, zs, tps, requests, items, rows, passages, squares):
    local_slots, cap, width = passages.shape
    blocks = (xs * tps * (GROUP + 2), LANES)
    return pl.pallas_call(
        functools.partial(score_kernel, local_slots, xs, zs, requests, items),
        out_shape=jax.ShapeDtypeStruct(blocks, jnp.bfloat16),
        in_specs=[VMEM, VMEM, VMEM],
        out_specs=VMEM,
        scratch_shapes=[
            pltpu.VMEM(blocks, jnp.float32),
        ],
        name="score",
        compiler_params=PARAMS,
    )(rows, passages.reshape(local_slots * cap, width), squares)


def merge(xs, zs, tps, got):
    return pl.pallas_call(
        functools.partial(merge_kernel, xs, tps),
        out_shape=(
            jax.ShapeDtypeStruct((zs * xs // 2, LANES), jnp.float32),
            jax.ShapeDtypeStruct((GROUP, LANES), jnp.float32),
        ),
        in_specs=[VMEM],
        out_specs=(VMEM, VMEM),
        scratch_shapes=[
            pltpu.VMEM((got.shape[0] + GROUP, LANES), jnp.float32),
            pltpu.VMEM((zs * xs // 2 + GROUP, LANES), jnp.float32),
        ],
        name="merge",
        compiler_params=PARAMS,
    )(got)


def finish(requests, nprobe, part, select, got, squares):
    return pl.pallas_call(
        finish_kernel,
        out_shape=jax.ShapeDtypeStruct((requests, nprobe, part), jnp.float32),
        in_specs=[VMEM, VMEM, VMEM],
        out_specs=VMEM,
        name="finish",
        compiler_params=PARAMS,
    )(select, got, squares)


def per_device(xs, zs, tps, hidden, latents, lengths, probes, cluster_slot, slab_sizes, passages):
    local_slots, cap, _ = passages.shape
    requests, nprobe = probes.shape
    payload, squares, select = pool(
        local_slots, xs, zs, tps, lengths, probes, cluster_slot, slab_sizes, hidden, latents
    )
    blocks = lax.all_to_all(payload, "z", 0, 0, tiled=True)
    blocks = spread(xs, zs, blocks.reshape(-1, LANES))
    rows = lax.all_to_all(blocks, "x", 0, 0, tiled=True).reshape(-1, LANES)
    partial = score(xs, zs, tps, requests, requests * nprobe, rows, passages, squares)
    blocks = lax.all_to_all(partial.reshape(xs * tps, -1, 2, LANES), ("x", "tp"), 0, 0, tiled=True)
    columns, squares = merge(xs, zs, tps, blocks.reshape(partial.shape))
    got = lax.all_to_all(columns.reshape(zs, 1, -1), "z", 0, 0, tiled=True)
    return finish(requests, nprobe, cap // tps, select, got.reshape(columns.shape), squares)


def solution(mesh):
    tps = mesh.shape["tp"]
    zs = mesh.shape["shard"] // XS
    fine = Mesh(mesh.devices.reshape(XS, zs, tps), ("x", "z", "tp"))
    shard = ("x", "z")
    placed = (
        P(shard, "tp"),
        P(None, "tp"),
        P(shard, None),
        P(shard, None),
        P(),
        P(),
        P(shard, None, "tp"),
    )
    return jax.shard_map(
        functools.partial(per_device, XS, zs, tps),
        mesh=fine,
        in_specs=placed,
        out_specs=P(shard, None, "tp"),
        check_vma=False,
    )
```

```python
import functools
import math

import jax
import jax.numpy as jnp
from jax import lax
from jax.experimental import pallas as pl
from jax.experimental.pallas import tpu as pltpu
from jax.sharding import Mesh
from jax.sharding import PartitionSpec as P

MOST = 4
LANES = 128
GROUP = 8
XS = 4
PACK_ROWS = 18
VMEM = pl.BlockSpec(memory_space=pltpu.VMEM)
HBM = pl.BlockSpec(memory_space=pltpu.HBM)
NT = (((1,), (1,)), ((), ()))
PARAMS = pltpu.CompilerParams(vmem_limit_bytes=16 << 20)


def three_parts(value):
    hi = value.astype(jnp.bfloat16).astype(jnp.float32)
    rest = value - hi
    mid = rest.astype(jnp.bfloat16).astype(jnp.float32)
    return hi, mid, rest - mid


def pool_kernel(
    local_slots, xs, zs, tps, lens_hbm, probes_hbm, slot_hbm, size_hbm, hid_hbm, lat_hbm,
    pay_ref, ss_ref, sel_ref,
    halves, count, lens_ref, probes_ref, slot_ref, size_ref, hid_ref, lat_ref, sems,
):
    tokens, width = hid_ref.shape
    requests, nprobe = probes_ref.shape
    pieces = width // LANES
    pairs = pieces // 2
    bits = local_slots.bit_length() - 1
    copies = [
        pltpu.make_async_copy(source, target, sems.at[i])
        for i, (source, target) in enumerate(
            [
                (probes_hbm, probes_ref),
                (slot_hbm, slot_ref),
                (lens_hbm, lens_ref),
                (size_hbm, size_ref),
                (lat_hbm, lat_ref),
                (hid_hbm, hid_ref),
            ]
        )
    ]
    for copy in copies:
        copy.start()
    for owner in range(xs * zs):
        count[owner] = 0
    for copy in copies[:4]:
        copy.wait()

    spot = lax.broadcasted_iota(jnp.int32, (1, LANES), 1)
    part = LANES // tps
    column = (spot & (part - 1)) + lax.axis_index("tp") * part
    group_of = lax.shift_right_logical(spot, part.bit_length() - 1)
    items = requests * nprobe
    lane = lax.broadcasted_iota(jnp.int32, (2, LANES), 1)
    marks = jnp.full((2, LANES), -1, jnp.int32)
    for query in range(requests):
        for j in range(nprobe):
            item = query * nprobe + j
            cluster = probes_ref[query, j]
            slot = slot_ref[cluster]
            owner = lax.shift_right_logical(slot, bits)
            rank = jnp.minimum(count[owner], MOST - 1)
            count[owner] = rank + 1
            place = owner * MOST + rank
            x, z = lax.shift_right_logical(owner, zs.bit_length() - 1), owner & (zs - 1)
            row = z * (xs // 2) + lax.shift_right_logical(x, 1)
            here = (group_of == (x & 1) * MOST + rank) & (column < size_ref[cluster])
            sel_ref[item : item + 1, :LANES] = jnp.where(spot == row, 1.0, 0.0)
            sel_ref[item : item + 1, LANES:] = jnp.where(here, 1.0, 0.0)
            code = (query << bits) + (slot & (local_slots - 1))
            marks = jnp.where(lane == item, place, jnp.where(lane == items + item, code, marks))
    marks = marks.astype(jnp.float32).astype(jnp.bfloat16)
    for copy in copies[4:]:
        copy.wait()

    row_id = lax.broadcasted_iota(jnp.int32, (GROUP, tokens), 0)
    position = lax.broadcasted_iota(jnp.int32, (GROUP, tokens), 1)
    begin = jnp.zeros((GROUP, tokens), jnp.int32)
    end = jnp.zeros((GROUP, tokens), jnp.int32)
    length_id = lax.broadcasted_iota(jnp.int32, (GROUP, width), 0)
    length = jnp.ones((GROUP, width), jnp.int32)
    start = jnp.int32(0)
    for r in range(requests):
        n = lens_ref[0, r]
        begin = jnp.where(row_id == r, start, begin)
        end = jnp.where(row_id == r, start + n, end)
        length = jnp.where(length_id == r, n, length)
        start = start + n
    member = jnp.where((position >= begin) & (position < end), 1.0, 0.0).astype(jnp.bfloat16)
    lat = lat_ref[...]
    logits = lax.dot_general(hid_ref[...], lat, NT, preferred_element_type=jnp.float32)
    top = jnp.max(logits, axis=1, keepdims=True)
    e = jnp.exp2((logits - top) * (math.log2(math.e) / math.sqrt(width)))
    weights = (e * (1.0 / jnp.sum(e, axis=1, keepdims=True))).astype(jnp.bfloat16)
    total = jnp.dot(member, weights, preferred_element_type=jnp.float32)
    parts = jnp.concatenate([*three_parts(total), jnp.zeros_like(total)], axis=0).astype(jnp.bfloat16)
    sums = jnp.dot(parts, lat, preferred_element_type=jnp.float32)
    sums = sums[:GROUP] + sums[GROUP : 2 * GROUP] + sums[2 * GROUP : 3 * GROUP]
    pooled = sums / length.astype(jnp.float32)
    ss_ref[...] = jnp.broadcast_to(jnp.sum(pooled * pooled, axis=1, keepdims=True), ss_ref.shape)

    for query in range(requests):
        for f in range(pieces):
            halves[query * pairs + f // 2, f % 2 : f % 2 + 1, :] = pooled[
                query : query + 1, f * LANES : (f + 1) * LANES
            ]
    rows = halves[...].astype(jnp.bfloat16)
    for place in range(pay_ref.shape[0]):
        pay_ref[place, : requests * pairs] = rows
        pay_ref[place, requests * pairs] = marks


def spread_kernel(got_ref, out_ref, rows):
    copies = out_ref.shape[0]
    packs = got_ref.shape[0] // PACK_ROWS
    rows[: got_ref.shape[0], :] = got_ref[...].astype(jnp.float32)
    pieces = [rows[pl.ds(i, packs, stride=PACK_ROWS), :] for i in range(PACK_ROWS - 1)]
    block = jnp.concatenate(pieces, axis=0).astype(jnp.bfloat16)
    for x in range(copies):
        out_ref[x] = block


def score_kernel(local_slots, xs, zs, requests, items, rows_ref, pas_ref, ss_ref, out_ref, blocks):
    owners = xs * zs
    cap = LANES
    pieces = pas_ref.shape[1] // LANES
    bits = local_slots.bit_length() - 1
    me = (lax.axis_index(("x", "z")) * MOST).astype(jnp.float32)

    def piece_of(i):
        starts = [x * (rows_ref.shape[0] // xs) + i * zs for x in range(xs)]
        return jnp.concatenate([rows_ref[r : r + zs, :] for r in starts], axis=0).astype(jnp.float32)

    marks = piece_of(requests * pieces)
    lane = lax.broadcasted_iota(jnp.int32, marks.shape, 1)
    place = jnp.where(lane < items, marks, -1.0)
    code = pltpu.roll(marks, LANES - items, 1)
    mine = jnp.concatenate([jnp.where(place == me + float(k), code, 0.0) for k in range(MOST)], axis=0)
    code = jnp.broadcast_to(jnp.sum(mine, axis=1, keepdims=True), mine.shape).astype(jnp.int32)
    pieces_of = [[piece_of(q * pieces + f) for f in range(pieces)] for q in range(requests)]
    chosen = []
    for k in range(MOST):
        query = lax.shift_right_logical(code[k * owners : (k + 1) * owners], bits)
        piece = []
        for f in range(pieces):
            got = pieces_of[0][f]
            for q in range(1, requests):
                got = jnp.where(query == q, pieces_of[q][f], got)
            piece.append(got)
        chosen.append(jnp.concatenate(piece, axis=1))
    chosen = jnp.concatenate(chosen, axis=0).astype(jnp.bfloat16)
    local = code & (local_slots - 1)
    total = jnp.zeros((MOST * owners, cap), jnp.float32)
    for s in range(0, local_slots, 2):
        got = lax.dot_general(
            chosen, pas_ref[s * cap : (s + 2) * cap, :], NT, preferred_element_type=jnp.float32
        )
        total = jnp.where(local == s, got[:, :cap], total)
        total = jnp.where(local == s + 1, got[:, cap:], total)

    tps = zs // GROUP * MOST
    part = LANES // tps
    height = out_ref.shape[0] // (xs * tps)
    lane = lax.broadcasted_iota(jnp.int32, (GROUP, LANES), 1)
    for x in range(xs):
        first = [k * owners + x * zs + h * GROUP for h in range(zs // GROUP) for k in range(MOST)]
        skew = [total[r : r + GROUP] for r in first]
        skew = [pltpu.roll(v, part * g, 1) if g else v for g, v in enumerate(skew)]
        for t in range(tps):
            mixed = skew[0]
            for g in range(1, tps):
                mixed = jnp.where(lane // part == (t + g) % tps, skew[g], mixed)
            row = (x * tps + t) * height
            blocks[row : row + GROUP, :] = mixed
    lane = lax.broadcasted_iota(jnp.int32, (1, LANES), 1)
    squares = ss_ref[0:1, :]
    for q in range(1, requests):
        squares = jnp.where(lane % (LANES // 2) // part == q, ss_ref[q : q + 1, :], squares)
    hi, mid, low = three_parts(squares)
    parts = jnp.concatenate([jnp.where(lane < LANES // 2, hi, mid), low], axis=0)
    for i in range(xs * tps):
        blocks[i * height + GROUP : (i + 1) * height, :] = parts
    out_ref[...] = blocks[...].astype(jnp.bfloat16)


def merge_kernel(xs, tps, got_ref, out_ref, ss_ref, blocks, columns):
    height = got_ref.shape[0] // (xs * tps)
    blocks[: got_ref.shape[0], :] = got_ref[...].astype(jnp.float32)
    total = []
    for x in range(xs):
        acc = blocks[x * tps * height : x * tps * height + GROUP, :]
        for t in range(1, tps):
            row = (x * tps + t) * height
            acc = acc + blocks[row : row + GROUP, :]
        turn = LANES - lax.axis_index("tp") * (LANES // tps)
        total.append(pltpu.roll(acc, turn, 1))
    left = lax.broadcasted_iota(jnp.int32, (GROUP, LANES), 1) < LANES // 2
    halves = xs // 2
    for r in range(halves):
        one, two = total[2 * r], total[2 * r + 1]
        near = jnp.where(left, one, pltpu.roll(two, LANES // 2, 1))
        far = jnp.where(left, pltpu.roll(one, LANES // 2, 1), two)
        columns[pl.ds(r, GROUP, stride=halves), :] = near
        columns[pl.ds(GROUP * halves + r, GROUP, stride=halves), :] = far
    out_ref[...] = columns[: out_ref.shape[0], :]
    mine = lax.axis_index("x") * (tps * height) + GROUP
    top = blocks[pl.ds(mine, 1), :]
    low = blocks[pl.ds(mine + 1, 1), :]
    for t in range(1, tps):
        top = top + blocks[pl.ds(mine + t * height, 1), :]
        low = low + blocks[pl.ds(mine + t * height + 1, 1), :]
    ss_ref[...] = jnp.broadcast_to(top + pltpu.roll(top, LANES // 2, 1) + low, ss_ref.shape)


def finish_kernel(sel_ref, got_ref, ss_ref, out_ref):
    requests, nprobe, part = out_ref.shape
    height = got_ref.shape[0]
    one_hot = sel_ref[:, :height].astype(jnp.bfloat16)
    parts = jnp.concatenate(three_parts(got_ref[...]), axis=1).astype(jnp.bfloat16)
    rows = jnp.dot(one_hot, parts, preferred_element_type=jnp.float32)
    rows = rows[:, :LANES] + rows[:, LANES : 2 * LANES] + rows[:, 2 * LANES :]
    rows = jnp.where(sel_ref[:, LANES:] > 0.0, rows, 0.0)
    step = LANES // 2
    while step >= part:
        rows = rows + pltpu.roll(rows, step, 1)
        step //= 2
    norm = jnp.sqrt(ss_ref[...] + 1e-06)
    for q in range(requests):
        here = pltpu.roll(norm, LANES - part * q, 1) if q else norm
        out_ref[q] = (rows[q * nprobe : (q + 1) * nprobe, :] / here)[:, :part]


def pool(local_slots, xs, zs, tps, lengths, probes, cluster_slot, slab_sizes, hidden, latents):
    pairs = hidden.shape[1] // LANES // 2
    whole = jnp.int32
    operands = (lengths, probes, cluster_slot, slab_sizes, hidden, latents)
    return pl.pallas_call(
        functools.partial(pool_kernel, local_slots, xs, zs, tps),
        out_shape=(
            jax.ShapeDtypeStruct((zs, probes.shape[0] * pairs + 1, 2, LANES), jnp.bfloat16),
            jax.ShapeDtypeStruct((GROUP, LANES), jnp.float32),
            jax.ShapeDtypeStruct((probes.size, 2 * LANES), jnp.float32),
        ),
        in_specs=[HBM] * len(operands),
        out_specs=(VMEM, VMEM, VMEM),
        scratch_shapes=[
            pltpu.VMEM((probes.shape[0] * pairs, 2, LANES), jnp.float32),
            pltpu.SMEM((xs * zs,), whole),
            pltpu.SMEM(lengths.shape, whole),
            pltpu.SMEM(probes.shape, whole),
            pltpu.SMEM(cluster_slot.shape, whole),
            pltpu.SMEM(slab_sizes.shape, whole),
            pltpu.VMEM(hidden.shape, hidden.dtype),
            pltpu.VMEM(latents.shape, latents.dtype),
            pltpu.SemaphoreType.DMA((len(operands),)),
        ],
        name="pool",
        compiler_params=PARAMS,
    )(*(pltpu.with_memory_space_constraint(x, pltpu.HBM) for x in operands))


def spread(xs, zs, got):
    return pl.pallas_call(
        spread_kernel,
        out_shape=jax.ShapeDtypeStruct((xs, zs * (PACK_ROWS - 1), LANES), jnp.bfloat16),
        in_specs=[VMEM],
        out_specs=VMEM,
        scratch_shapes=[pltpu.VMEM((got.shape[0] + 3 * GROUP, LANES), jnp.float32)],
        name="spread",
        compiler_params=PARAMS,
    )(got)


def score(xs, zs, tps, requests, items, rows, passages, squares):
    local_slots, cap, width = passages.shape
    blocks = (xs * tps * (GROUP + 2), LANES)
    return pl.pallas_call(
        functools.partial(score_kernel, local_slots, xs, zs, requests, items),
        out_shape=jax.ShapeDtypeStruct(blocks, jnp.bfloat16),
        in_specs=[VMEM, VMEM, VMEM],
        out_specs=VMEM,
        scratch_shapes=[
            pltpu.VMEM(blocks, jnp.float32),
        ],
        name="score",
        compiler_params=PARAMS,
    )(rows, passages.reshape(local_slots * cap, width), squares)


def merge(xs, zs, tps, got):
    return pl.pallas_call(
        functools.partial(merge_kernel, xs, tps),
        out_shape=(
            jax.ShapeDtypeStruct((zs * xs // 2, LANES), jnp.float32),
            jax.ShapeDtypeStruct((GROUP, LANES), jnp.float32),
        ),
        in_specs=[VMEM],
        out_specs=(VMEM, VMEM),
        scratch_shapes=[
            pltpu.VMEM((got.shape[0] + GROUP, LANES), jnp.float32),
            pltpu.VMEM((zs * xs // 2 + GROUP, LANES), jnp.float32),
        ],
        name="merge",
        compiler_params=PARAMS,
    )(got)


def finish(requests, nprobe, part, select, got, squares):
    return pl.pallas_call(
        finish_kernel,
        out_shape=jax.ShapeDtypeStruct((requests, nprobe, part), jnp.float32),
        in_specs=[VMEM, VMEM, VMEM],
        out_specs=VMEM,
        name="finish",
        compiler_params=PARAMS,
    )(select, got, squares)


def per_device(xs, zs, tps, hidden, latents, lengths, probes, cluster_slot, slab_sizes, passages):
    local_slots, cap, _ = passages.shape
    requests, nprobe = probes.shape
    payload, squares, select = pool(
        local_slots, xs, zs, tps, lengths, probes, cluster_slot, slab_sizes, hidden, latents
    )
    blocks = lax.all_to_all(payload, "z", 0, 0, tiled=True)
    blocks = spread(xs, zs, blocks.reshape(-1, LANES))
    rows = lax.all_to_all(blocks, "x", 0, 0, tiled=True).reshape(-1, LANES)
    partial = score(xs, zs, tps, requests, requests * nprobe, rows, passages, squares)
    blocks = lax.all_to_all(partial.reshape(xs * tps, -1, 2, LANES), ("x", "tp"), 0, 0, tiled=True)
    columns, squares = merge(xs, zs, tps, blocks.reshape(partial.shape))
    got = lax.all_to_all(columns.reshape(zs, 1, -1), "z", 0, 0, tiled=True)
    return finish(requests, nprobe, cap // tps, select, got.reshape(columns.shape), squares)


def solution(mesh):
    tps = mesh.shape["tp"]
    zs = mesh.shape["shard"] // XS
    fine = Mesh(mesh.devices.reshape(XS, zs, tps), ("x", "z", "tp"))
    shard = ("x", "z")
    placed = (
        P(shard, "tp"),
        P(None, "tp"),
        P(shard, None),
        P(shard, None),
        P(),
        P(),
        P(shard, None, "tp"),
    )
    return jax.shard_map(
        functools.partial(per_device, XS, zs, tps),
        mesh=fine,
        in_specs=placed,
        out_specs=P(shard, None, "tp"),
        check_vma=False,
    )
```

```python
import functools
import math

import jax
import jax.numpy as jnp
from jax import lax
from jax.experimental import pallas as pl
from jax.experimental.pallas import tpu as pltpu
from jax.sharding import Mesh
from jax.sharding import PartitionSpec as P

MOST = 4
LANES = 128
GROUP = 8
XS = 4
PACK_ROWS = 18
VMEM = pl.BlockSpec(memory_space=pltpu.VMEM)
HBM = pl.BlockSpec(memory_space=pltpu.HBM)
NT = (((1,), (1,)), ((), ()))
PARAMS = pltpu.CompilerParams(vmem_limit_bytes=16 << 20)


def three_parts(value):
    hi = value.astype(jnp.bfloat16).astype(jnp.float32)
    rest = value - hi
    mid = rest.astype(jnp.bfloat16).astype(jnp.float32)
    return hi, mid, rest - mid


def pool_kernel(
    local_slots, xs, zs, tps, lens_hbm, probes_hbm, slot_hbm, size_hbm, hid_hbm, lat_hbm,
    pay_ref, ss_ref, sel_ref,
    halves, count, lens_ref, probes_ref, slot_ref, size_ref, hid_ref, lat_ref, sems,
):
    tokens, width = hid_ref.shape
    requests, nprobe = probes_ref.shape
    pieces = width // LANES
    pairs = pieces // 2
    bits = local_slots.bit_length() - 1
    copies = [
        pltpu.make_async_copy(source, target, sems.at[i])
        for i, (source, target) in enumerate(
            [
                (probes_hbm, probes_ref),
                (slot_hbm, slot_ref),
                (lens_hbm, lens_ref),
                (size_hbm, size_ref),
                (lat_hbm, lat_ref),
                (hid_hbm, hid_ref),
            ]
        )
    ]
    for copy in copies:
        copy.start()
    for owner in range(xs * zs):
        count[owner] = 0
    for copy in copies[:4]:
        copy.wait()

    spot = lax.broadcasted_iota(jnp.int32, (1, LANES), 1)
    part = LANES // tps
    column = (spot & (part - 1)) + lax.axis_index("tp") * part
    group_of = lax.shift_right_logical(spot, part.bit_length() - 1)
    items = requests * nprobe
    lane = lax.broadcasted_iota(jnp.int32, (2, LANES), 1)
    marks = jnp.full((2, LANES), -1, jnp.int32)
    for query in range(requests):
        for j in range(nprobe):
            item = query * nprobe + j
            cluster = probes_ref[query, j]
            slot = slot_ref[cluster]
            owner = lax.shift_right_logical(slot, bits)
            rank = jnp.minimum(count[owner], MOST - 1)
            count[owner] = rank + 1
            place = owner * MOST + rank
            x, z = lax.shift_right_logical(owner, zs.bit_length() - 1), owner & (zs - 1)
            row = z * (xs // 2) + lax.shift_right_logical(x, 1)
            here = (group_of == (x & 1) * MOST + rank) & (column < size_ref[cluster])
            sel_ref[item : item + 1, :LANES] = jnp.where(spot == row, 1.0, 0.0)
            sel_ref[item : item + 1, LANES:] = jnp.where(here, 1.0, 0.0)
            code = (query << bits) + (slot & (local_slots - 1))
            marks = jnp.where(lane == item, place, jnp.where(lane == items + item, code, marks))
    marks = marks.astype(jnp.float32).astype(jnp.bfloat16)
    for copy in copies[4:]:
        copy.wait()

    row_id = lax.broadcasted_iota(jnp.int32, (GROUP, tokens), 0)
    position = lax.broadcasted_iota(jnp.int32, (GROUP, tokens), 1)
    begin = jnp.zeros((GROUP, tokens), jnp.int32)
    end = jnp.zeros((GROUP, tokens), jnp.int32)
    length_id = lax.broadcasted_iota(jnp.int32, (GROUP, width), 0)
    length = jnp.ones((GROUP, width), jnp.int32)
    start = jnp.int32(0)
    for r in range(requests):
        n = lens_ref[0, r]
        begin = jnp.where(row_id == r, start, begin)
        end = jnp.where(row_id == r, start + n, end)
        length = jnp.where(length_id == r, n, length)
        start = start + n
    member = jnp.where((position >= begin) & (position < end), 1.0, 0.0).astype(jnp.bfloat16)
    lat = lat_ref[...]
    logits = lax.dot_general(hid_ref[...], lat, NT, preferred_element_type=jnp.float32)
    top = jnp.max(logits, axis=1, keepdims=True)
    e = jnp.exp2((logits - top) * (math.log2(math.e) / math.sqrt(width)))
    weights = (e * (1.0 / jnp.sum(e, axis=1, keepdims=True))).astype(jnp.bfloat16)
    total = jnp.dot(member, weights, preferred_element_type=jnp.float32)
    parts = jnp.concatenate([*three_parts(total), jnp.zeros_like(total)], axis=0).astype(jnp.bfloat16)
    sums = jnp.dot(parts, lat, preferred_element_type=jnp.float32)
    sums = sums[:GROUP] + sums[GROUP : 2 * GROUP] + sums[2 * GROUP : 3 * GROUP]
    pooled = sums / length.astype(jnp.float32)
    ss_ref[...] = jnp.broadcast_to(jnp.sum(pooled * pooled, axis=1, keepdims=True), ss_ref.shape)

    for query in range(requests):
        for f in range(pieces):
            halves[query * pairs + f // 2, f % 2 : f % 2 + 1, :] = pooled[
                query : query + 1, f * LANES : (f + 1) * LANES
            ]
    rows = halves[...].astype(jnp.bfloat16)
    for place in range(pay_ref.shape[0]):
        pay_ref[place, : requests * pairs] = rows
        pay_ref[place, requests * pairs] = marks


def spread_kernel(got_ref, out_ref, rows):
    copies = out_ref.shape[0]
    packs = got_ref.shape[0] // PACK_ROWS
    rows[: got_ref.shape[0], :] = got_ref[...].astype(jnp.float32)
    pieces = [rows[pl.ds(i, packs, stride=PACK_ROWS), :] for i in range(PACK_ROWS - 1)]
    block = jnp.concatenate(pieces, axis=0).astype(jnp.bfloat16)
    for x in range(copies):
        out_ref[x] = block


def score_kernel(local_slots, xs, zs, requests, items, rows_ref, pas_ref, ss_ref, out_ref, blocks):
    owners = xs * zs
    cap = LANES
    pieces = pas_ref.shape[1] // LANES
    bits = local_slots.bit_length() - 1
    me = (lax.axis_index(("x", "z")) * MOST).astype(jnp.float32)

    def piece_of(i):
        starts = [x * (rows_ref.shape[0] // xs) + i * zs for x in range(xs)]
        return jnp.concatenate([rows_ref[r : r + zs, :] for r in starts], axis=0)

    marks = piece_of(requests * pieces).astype(jnp.float32)
    lane = lax.broadcasted_iota(jnp.int32, marks.shape, 1)
    place = jnp.where(lane < items, marks, -1.0)
    code = pltpu.roll(marks, LANES - items, 1)
    mine = jnp.concatenate([jnp.where(place == me + float(k), code, 0.0) for k in range(MOST)], axis=0)
    code = jnp.broadcast_to(jnp.sum(mine, axis=1, keepdims=True), mine.shape).astype(jnp.int32)
    pieces_of = [[piece_of(q * pieces + f) for f in range(pieces)] for q in range(requests)]
    chosen = []
    for k in range(MOST):
        query = lax.shift_right_logical(code[k * owners : (k + 1) * owners], bits)
        query = query.astype(jnp.float32).astype(jnp.bfloat16)
        piece = []
        for f in range(pieces):
            got = pieces_of[0][f]
            for q in range(1, requests):
                got = jnp.where(query == jnp.bfloat16(q), pieces_of[q][f], got)
            piece.append(got)
        chosen.append(jnp.concatenate(piece, axis=1))
    chosen = jnp.concatenate(chosen, axis=0)
    local = code & (local_slots - 1)
    total = jnp.zeros((MOST * owners, cap), jnp.float32)
    for s in range(0, local_slots, 2):
        got = lax.dot_general(
            chosen, pas_ref[s * cap : (s + 2) * cap, :], NT, preferred_element_type=jnp.float32
        )
        total = jnp.where(local == s, got[:, :cap], total)
        total = jnp.where(local == s + 1, got[:, cap:], total)

    tps = zs // GROUP * MOST
    part = LANES // tps
    height = out_ref.shape[0] // (xs * tps)
    lane = lax.broadcasted_iota(jnp.int32, (GROUP, LANES), 1)
    for x in range(xs):
        first = [k * owners + x * zs + h * GROUP for h in range(zs // GROUP) for k in range(MOST)]
        skew = [total[r : r + GROUP] for r in first]
        skew = [pltpu.roll(v, part * g, 1) if g else v for g, v in enumerate(skew)]
        for t in range(tps):
            mixed = skew[0]
            for g in range(1, tps):
                mixed = jnp.where(lane // part == (t + g) % tps, skew[g], mixed)
            row = (x * tps + t) * height
            blocks[row : row + GROUP, :] = mixed
    lane = lax.broadcasted_iota(jnp.int32, (1, LANES), 1)
    squares = ss_ref[0:1, :]
    for q in range(1, requests):
        squares = jnp.where(lane % (LANES // 2) // part == q, ss_ref[q : q + 1, :], squares)
    hi, mid, low = three_parts(squares)
    parts = jnp.concatenate([jnp.where(lane < LANES // 2, hi, mid), low], axis=0)
    for i in range(xs * tps):
        blocks[i * height + GROUP : (i + 1) * height, :] = parts
    out_ref[...] = blocks[...].astype(jnp.bfloat16)


def merge_kernel(xs, tps, got_ref, out_ref, ss_ref, blocks, columns):
    height = got_ref.shape[0] // (xs * tps)
    blocks[: got_ref.shape[0], :] = got_ref[...].astype(jnp.float32)
    total = []
    for x in range(xs):
        acc = blocks[x * tps * height : x * tps * height + GROUP, :]
        for t in range(1, tps):
            row = (x * tps + t) * height
            acc = acc + blocks[row : row + GROUP, :]
        turn = LANES - lax.axis_index("tp") * (LANES // tps)
        total.append(pltpu.roll(acc, turn, 1))
    left = lax.broadcasted_iota(jnp.int32, (GROUP, LANES), 1) < LANES // 2
    halves = xs // 2
    for r in range(halves):
        one, two = total[2 * r], total[2 * r + 1]
        near = jnp.where(left, one, pltpu.roll(two, LANES // 2, 1))
        far = jnp.where(left, pltpu.roll(one, LANES // 2, 1), two)
        columns[pl.ds(r, GROUP, stride=halves), :] = near
        columns[pl.ds(GROUP * halves + r, GROUP, stride=halves), :] = far
    out_ref[...] = columns[: out_ref.shape[0], :]
    mine = lax.axis_index("x") * (tps * height) + GROUP
    top = blocks[pl.ds(mine, 1), :]
    low = blocks[pl.ds(mine + 1, 1), :]
    for t in range(1, tps):
        top = top + blocks[pl.ds(mine + t * height, 1), :]
        low = low + blocks[pl.ds(mine + t * height + 1, 1), :]
    ss_ref[...] = jnp.broadcast_to(top + pltpu.roll(top, LANES // 2, 1) + low, ss_ref.shape)


def finish_kernel(sel_ref, got_ref, ss_ref, out_ref):
    requests, nprobe, part = out_ref.shape
    height = got_ref.shape[0]
    one_hot = sel_ref[:, :height].astype(jnp.bfloat16)
    parts = jnp.concatenate(three_parts(got_ref[...]), axis=1).astype(jnp.bfloat16)
    rows = jnp.dot(one_hot, parts, preferred_element_type=jnp.float32)
    rows = rows[:, :LANES] + rows[:, LANES : 2 * LANES] + rows[:, 2 * LANES :]
    rows = jnp.where(sel_ref[:, LANES:] > 0.0, rows, 0.0)
    step = LANES // 2
    while step >= part:
        rows = rows + pltpu.roll(rows, step, 1)
        step //= 2
    norm = jnp.sqrt(ss_ref[...] + 1e-06)
    for q in range(requests):
        here = pltpu.roll(norm, LANES - part * q, 1) if q else norm
        out_ref[q] = (rows[q * nprobe : (q + 1) * nprobe, :] / here)[:, :part]


def pool(local_slots, xs, zs, tps, lengths, probes, cluster_slot, slab_sizes, hidden, latents):
    pairs = hidden.shape[1] // LANES // 2
    whole = jnp.int32
    operands = (lengths, probes, cluster_slot, slab_sizes, hidden, latents)
    return pl.pallas_call(
        functools.partial(pool_kernel, local_slots, xs, zs, tps),
        out_shape=(
            jax.ShapeDtypeStruct((zs, probes.shape[0] * pairs + 1, 2, LANES), jnp.bfloat16),
            jax.ShapeDtypeStruct((GROUP, LANES), jnp.float32),
            jax.ShapeDtypeStruct((probes.size, 2 * LANES), jnp.float32),
        ),
        in_specs=[HBM] * len(operands),
        out_specs=(VMEM, VMEM, VMEM),
        scratch_shapes=[
            pltpu.VMEM((probes.shape[0] * pairs, 2, LANES), jnp.float32),
            pltpu.SMEM((xs * zs,), whole),
            pltpu.SMEM(lengths.shape, whole),
            pltpu.SMEM(probes.shape, whole),
            pltpu.SMEM(cluster_slot.shape, whole),
            pltpu.SMEM(slab_sizes.shape, whole),
            pltpu.VMEM(hidden.shape, hidden.dtype),
            pltpu.VMEM(latents.shape, latents.dtype),
            pltpu.SemaphoreType.DMA((len(operands),)),
        ],
        name="pool",
        compiler_params=PARAMS,
    )(*(pltpu.with_memory_space_constraint(x, pltpu.HBM) for x in operands))


def spread(xs, zs, got):
    return pl.pallas_call(
        spread_kernel,
        out_shape=jax.ShapeDtypeStruct((xs, zs * (PACK_ROWS - 1), LANES), jnp.bfloat16),
        in_specs=[VMEM],
        out_specs=VMEM,
        scratch_shapes=[pltpu.VMEM((got.shape[0] + 3 * GROUP, LANES), jnp.float32)],
        name="spread",
        compiler_params=PARAMS,
    )(got)


def score(xs, zs, tps, requests, items, rows, passages, squares):
    local_slots, cap, width = passages.shape
    blocks = (xs * tps * (GROUP + 2), LANES)
    return pl.pallas_call(
        functools.partial(score_kernel, local_slots, xs, zs, requests, items),
        out_shape=jax.ShapeDtypeStruct(blocks, jnp.bfloat16),
        in_specs=[VMEM, VMEM, VMEM],
        out_specs=VMEM,
        scratch_shapes=[
            pltpu.VMEM(blocks, jnp.float32),
        ],
        name="score",
        compiler_params=PARAMS,
    )(rows, passages.reshape(local_slots * cap, width), squares)


def merge(xs, zs, tps, got):
    return pl.pallas_call(
        functools.partial(merge_kernel, xs, tps),
        out_shape=(
            jax.ShapeDtypeStruct((zs * xs // 2, LANES), jnp.float32),
            jax.ShapeDtypeStruct((GROUP, LANES), jnp.float32),
        ),
        in_specs=[VMEM],
        out_specs=(VMEM, VMEM),
        scratch_shapes=[
            pltpu.VMEM((got.shape[0] + GROUP, LANES), jnp.float32),
            pltpu.VMEM((zs * xs // 2 + GROUP, LANES), jnp.float32),
        ],
        name="merge",
        compiler_params=PARAMS,
    )(got)


def finish(requests, nprobe, part, select, got, squares):
    return pl.pallas_call(
        finish_kernel,
        out_shape=jax.ShapeDtypeStruct((requests, nprobe, part), jnp.float32),
        in_specs=[VMEM, VMEM, VMEM],
        out_specs=VMEM,
        name="finish",
        compiler_params=PARAMS,
    )(select, got, squares)


def per_device(xs, zs, tps, hidden, latents, lengths, probes, cluster_slot, slab_sizes, passages):
    local_slots, cap, _ = passages.shape
    requests, nprobe = probes.shape
    payload, squares, select = pool(
        local_slots, xs, zs, tps, lengths, probes, cluster_slot, slab_sizes, hidden, latents
    )
    blocks = lax.all_to_all(payload, "z", 0, 0, tiled=True)
    blocks = spread(xs, zs, blocks.reshape(-1, LANES))
    rows = lax.all_to_all(blocks, "x", 0, 0, tiled=True).reshape(-1, LANES)
    partial = score(xs, zs, tps, requests, requests * nprobe, rows, passages, squares)
    blocks = lax.all_to_all(partial.reshape(xs * tps, -1, 2, LANES), ("x", "tp"), 0, 0, tiled=True)
    columns, squares = merge(xs, zs, tps, blocks.reshape(partial.shape))
    got = lax.all_to_all(columns.reshape(zs, 1, -1), "z", 0, 0, tiled=True)
    return finish(requests, nprobe, cap // tps, select, got.reshape(columns.shape), squares)


def solution(mesh):
    tps = mesh.shape["tp"]
    zs = mesh.shape["shard"] // XS
    fine = Mesh(mesh.devices.reshape(XS, zs, tps), ("x", "z", "tp"))
    shard = ("x", "z")
    placed = (
        P(shard, "tp"),
        P(None, "tp"),
        P(shard, None),
        P(shard, None),
        P(),
        P(),
        P(shard, None, "tp"),
    )
    return jax.shard_map(
        functools.partial(per_device, XS, zs, tps),
        mesh=fine,
        in_specs=placed,
        out_specs=P(shard, None, "tp"),
        check_vma=False,
    )
```
